256 devices in a mesh: row: 64 (over y, z, core), col: 4 (over x).
Axes of the slice: x: 4, y: 4, z: 8, core: 2. Of those that a mesh axis runs over, the one named last changes fastest.
Arguments:
- momentum: float32 [28672, 8192], P('row', 'col'), may hold values from -180 to 180, as said below
- grad: bfloat16 [28672, 8192], P('row', 'col'), may hold values from -6 to 6
- q_basis: float32 [8192, 512], P(('col', 'row')), may hold values from -6 to 6
Outputs:
- p_factor: float32 [28672, 512], P(('row', 'col'))
- q_next: float32 [8192, 512], P(('col', 'row'))
- momentum_next: float32 [28672, 8192], P('row', 'col')
The draws below stay inside these ranges and needn't reach their ends.
Inputs may be any that keep to these rules, and one draw needn't show every extreme that they name: momentum entries are values times a scale for each column.
All inputs are finite; a program needn't handle non-finite values.
Results may differ from the reference program's by a relative error of at most 0.00035.
The reference program's roundings to bfloat16 on the way (of `q_half`, `b_half`, `p_half` and `r_half`) count: a program that leaves them out, or rounds other values in their place, can miss the bound.
Values may be sent and summed in bfloat16 or wider, within the bound.
No kernel may reach another device: no remote copies, remote signals or barrier semaphores. Data moves between devices by JAX's collectives and lax.ppermute only.
A program may use at most 64 MiB of HBM per device.

```python
import jax
import jax.numpy as jnp
from jax import lax

ROWS = 28672
COLS = 8192
RANK = 512


def draw_momentum(key, part):
    key = jax.random.fold_in(key, 11)
    key_scale = jax.random.fold_in(key, 1)
    key_value = jax.random.fold_in(key, 2)
    spread = jnp.exp(jax.random.uniform(key_scale, (1, COLS), jnp.float32, 0.0, jnp.log(10.0)))
    rising = jnp.exp(jnp.log(3.0) * jnp.arange(COLS, dtype=jnp.float32) / COLS)[None, :]
    values = jax.random.truncated_normal(key_value, -6.0, 6.0, (ROWS, COLS), jnp.float32)
    return (values * spread * rising).astype(jnp.float32)


def block_scale(own_key, dims, pieces, smallest, top_value):
    def one(axis_at, parts):
        steps = jax.random.uniform(jax.random.fold_in(jax.random.fold_in(own_key, 6), axis_at), (parts,), jnp.float32, smallest / len(pieces), top_value / len(pieces))
        return jnp.repeat(jnp.exp(steps), dims[axis_at] // parts).reshape((-1,) + (1,) * (len(dims) - axis_at - 1))

    loudness = one(*pieces[0])
    for cut in pieces[1:]:
        loudness = loudness * one(*cut)
    return loudness


def bell_draw(stream_key, shape, width, bound, pieces=(), held_as=jnp.bfloat16):
    gain = block_scale(stream_key, shape, pieces, -0.22, 0.18) if pieces else 1.0
    array = jax.random.normal(stream_key, shape, jnp.float32) * width * gain
    return jnp.minimum(jnp.maximum(array, -bound), bound).astype(held_as)


def setup_inputs(seed: int = 0) -> dict:
    splits = jax.random.split(jax.random.key(seed), 4)
    return {
        "momentum": draw_momentum(jax.random.fold_in(splits[3], 71), 0),
        "grad": bell_draw(splits[1], (ROWS, COLS), 1.0, 6.0, ((0, 64), (1, 4))),
        "q_basis": bell_draw(splits[2], (COLS, RANK), 1.0, 6.0, ((0, 256),), jnp.float32),
    }


decay_gap = 0.05

def reference(momentum, grad, q_basis):
    q_half = q_basis.astype(jnp.bfloat16)
    mixed = momentum + grad.astype(jnp.float32)
    b_half = mixed.astype(jnp.bfloat16)
    product = jnp.dot(b_half.astype(jnp.float32), q_half.astype(jnp.float32), preferred_element_type=jnp.float32)
    gram = jnp.dot(product.T, product, precision=lax.Precision.HIGHEST)
    factor = jnp.linalg.cholesky(gram)
    p_orth = jax.scipy.linalg.solve_triangular(factor, product.T, lower=True).T
    p_factor = p_orth * jnp.sqrt(jnp.float32(ROWS))
    p_half = p_orth.astype(jnp.bfloat16)
    right = lax.dot_general(b_half.astype(jnp.float32), p_half.astype(jnp.float32), (((0,), (0,)), ((), ())), preferred_element_type=jnp.float32)
    col_power = lax.optimization_barrier(jnp.sum(right * right, axis=0))
    q_next = right * lax.rsqrt(col_power / COLS + 1e-06)
    r_half = right.astype(jnp.bfloat16)
    update = lax.dot_general(p_half.astype(jnp.float32), r_half.astype(jnp.float32), (((1,), (1,)), ((), ())), preferred_element_type=jnp.float32)
    momentum_next = mixed - decay_gap * update
    return (p_factor, q_next, momentum_next)
```

```python
import jax
import jax.numpy as jnp
import numpy as np
from jax import lax
from jax.experimental import pallas as pl
from jax.experimental.pallas import tpu as pltpu
from jax.sharding import Mesh, PartitionSpec as P

ROWS = 28672
COLS = 8192
RANK = 512
DECAY = 0.05

NY, NZ, NC, NX = 4, 8, 2, 4
ROW_LOCAL = ROWS // (NY * NZ * NC)
SHARE = ROW_LOCAL // NX
BLOCK = 512
PIECE = 32
F32, BF16 = jnp.float32, jnp.bfloat16
SIZES = {"y": NY, "z": NZ, "c": NC, "x": NX}
VMEM = pl.BlockSpec(memory_space=pltpu.VMEM)
SMEM = pl.BlockSpec(memory_space=pltpu.SMEM)
PARAMS = pltpu.CompilerParams(vmem_limit_bytes=48 * 1024 * 1024)
HIGH = lax.Precision.HIGHEST


def shift(x, axis, k):
    n = SIZES[axis]
    return lax.ppermute(x, axis, [(i, (i + k) % n) for i in range(n)])


def spread(x, axes, n):
    full = jnp.broadcast_to(x[None], (n,) + x.shape)
    return lax.all_to_all(full, axes, 0, 0, tiled=True)


def prep_kernel(place, m_ref, g_ref, b_ref):
    for k in range(NX):
        start = pl.multiple_of(lax.rem(place[0] + k, NX) * SHARE, SHARE)
        mixed = m_ref[pl.ds(start, SHARE), :] + g_ref[pl.ds(start, SHARE), :].astype(F32)
        b_ref[0, pl.ds(k * SHARE, SHARE), :] = mixed.astype(BF16)


def prep(place, momentum, grad):
    spec = pl.BlockSpec((ROW_LOCAL, BLOCK), lambda k, s: (0, lax.rem(s[1] + k, NY)))
    return pl.pallas_call(
        prep_kernel,
        grid_spec=pltpu.PrefetchScalarGridSpec(
            num_scalar_prefetch=1,
            grid=(NY,),
            in_specs=[spec, spec],
            out_specs=pl.BlockSpec((1, ROW_LOCAL, BLOCK), lambda k, s: (k, 0, 0)),
        ),
        out_shape=jax.ShapeDtypeStruct((NY, ROW_LOCAL, BLOCK), BF16),
        compiler_params=PARAMS,
    )(place, momentum, grad)


def weave(place, mine, other, whole):
    c = place[2]
    for z in range(NZ):
        at = pl.multiple_of(z * 2 * PIECE + c * PIECE, PIECE)
        whole[pl.ds(at, PIECE), :] = mine[pl.ds(z * PIECE, PIECE), :]
        at = pl.multiple_of(z * 2 * PIECE + (1 - c) * PIECE, PIECE)
        whole[pl.ds(at, PIECE), :] = other[pl.ds(z * PIECE, PIECE), :]


def product_kernel(place, b_ref, *refs):
    mine, other, out, whole = refs[:NY], refs[NY : 2 * NY], refs[2 * NY], refs[2 * NY + 1]
    for k in range(NY):
        weave(place, mine[k], other[k], whole.at[k])
    total = jnp.dot(b_ref[0], whole[0], preferred_element_type=F32)
    for k in range(1, NY):
        total += jnp.dot(b_ref[k], whole[k], preferred_element_type=F32)
    out[...] = total


def product_of(place, b, mine, other):
    return pl.pallas_call(
        product_kernel,
        in_specs=[SMEM] + [VMEM] * (1 + 2 * NY),
        out_specs=VMEM,
        out_shape=jax.ShapeDtypeStruct((ROW_LOCAL, RANK), F32),
        scratch_shapes=[pltpu.VMEM((NY, BLOCK, RANK), BF16)],
        compiler_params=PARAMS,
    )(place, b, *mine, *other)


def gram_kernel(p_ref, out):
    left, right = p_ref[:, :256], p_ref[:, 256:]
    dims = (((0,), (0,)), ((), ()))
    for i, (a, b) in enumerate(((left, left), (right, left), (right, right))):
        g = lax.dot_general(a, b, dims, precision=HIGH, preferred_element_type=F32)
        out[pl.ds(i * 512, 256), :] = g[:, :128]
        out[pl.ds(i * 512 + 256, 256), :] = g[:, 128:]


def gram_of(product):
    return pl.pallas_call(
        gram_kernel,
        in_specs=[VMEM],
        out_specs=VMEM,
        out_shape=jax.ShapeDtypeStruct((1536, 128), F32),
        compiler_params=PARAMS,
    )(product)


def right_kernel(place, w_ref, *refs):
    prod, b = refs[:NY], refs[NY : 2 * NY]
    p_own, p_factor, right, total = refs[2 * NY :]
    for k in range(NY):
        p = lax.dot_general(
            prod[k][...], w_ref[...], (((1,), (1,)), ((), ())), precision=HIGH, preferred_element_type=F32
        )
        half = p.astype(BF16)
        if k == 0:
            p_factor[...] = p[:SHARE] * jnp.sqrt(F32(ROWS))
            p_own[...] = half
        part = lax.dot_general(b[k][...], half, (((0,), (0,)), ((), ())), preferred_element_type=F32)
        if k == 0:
            total[...] = part
        else:
            total[...] += part
    c = place[2]
    for z in range(NZ):
        at = pl.multiple_of(z * 2 * PIECE + c * PIECE, PIECE)
        right[0, pl.ds(z * PIECE, PIECE), :] = total[pl.ds(at, PIECE), :]
        at = pl.multiple_of(z * 2 * PIECE + (1 - c) * PIECE, PIECE)
        right[1, pl.ds(z * PIECE, PIECE), :] = total[pl.ds(at, PIECE), :]


def right_of(place, w, prod, b):
    return pl.pallas_call(
        right_kernel,
        in_specs=[SMEM] + [VMEM] * (1 + 2 * NY),
        out_specs=[VMEM] * 3,
        out_shape=[
            jax.ShapeDtypeStruct((ROW_LOCAL, RANK), BF16),
            jax.ShapeDtypeStruct((SHARE, RANK), F32),
            jax.ShapeDtypeStruct((NC, NZ * PIECE, RANK), F32),
        ],
        scratch_shapes=[pltpu.VMEM((BLOCK, RANK), F32)],
        compiler_params=PARAMS,
    )(place, w, *prod, *b)


def update_kernel(place, p_ref, *refs):
    mine, other = refs[:NY], refs[NY : 2 * NY]
    m_ref, g_ref, out, whole = refs[2 * NY :]
    step = pl.program_id(0)
    for k in range(NY):

        @pl.when(step == k)
        def _():
            weave(place, mine[k], other[k], whole)

    update = lax.dot_general(
        p_ref[...], whole[...], (((1,), (1,)), ((), ())), preferred_element_type=F32
    )
    for k in range(NX):
        start = pl.multiple_of(lax.rem(place[0] + k, NX) * SHARE, SHARE)
        mixed = m_ref[pl.ds(start, SHARE), :] + g_ref[pl.ds(start, SHARE), :].astype(F32)
        out[pl.ds(start, SHARE), :] = mixed - DECAY * update[k * SHARE : (k + 1) * SHARE]


def update_of(place, p_own, mine, other, momentum, grad):
    spec = pl.BlockSpec((ROW_LOCAL, BLOCK), lambda k, s: (0, lax.rem(s[1] + k, NY)))
    return pl.pallas_call(
        update_kernel,
        grid_spec=pltpu.PrefetchScalarGridSpec(
            num_scalar_prefetch=1,
            grid=(NY,),
            in_specs=[VMEM] * (1 + 2 * NY) + [spec, spec],
            out_specs=spec,
            scratch_shapes=[pltpu.VMEM((BLOCK, RANK), BF16)],
        ),
        out_shape=jax.ShapeDtypeStruct((ROW_LOCAL, NY * BLOCK), F32),
        compiler_params=PARAMS,
    )(place, p_own, *mine, *other, momentum, grad)


def gather_rows(piece):
    own = spread(piece, "z", NZ).reshape(NZ * PIECE, RANK)
    mine = [own] + [shift(own, "y", -k) for k in range(1, NY)]
    other = [shift(v, "c", 1) for v in mine]
    return mine, other


def pair(c, mine, other):
    return jnp.where(c == 0, jnp.stack([mine, other]), jnp.stack([other, mine]))


def factor_inverse(blocks):
    a, b, d = (jnp.concatenate([v[:256], v[256:]], 1) for v in jnp.split(blocks, 3))
    gram = jnp.concatenate([jnp.concatenate([a, b.T], 1), jnp.concatenate([b, d], 1)], 0)
    factor = jnp.linalg.cholesky(gram)
    return jax.scipy.linalg.solve_triangular(factor, jnp.eye(RANK, dtype=F32), lower=True)


def body(momentum, grad, q_basis):
    x, y, c = lax.axis_index("x"), lax.axis_index("y"), lax.axis_index("c")
    place = jnp.stack([x, y, c]).astype(jnp.int32)

    q_mine, q_other = gather_rows(q_basis.astype(BF16))
    b = prep(place, momentum, grad)
    partial = product_of(place, b, q_mine, q_other).reshape(NX, SHARE, RANK)

    share = partial[0] + sum(shift(partial[k], "x", k) for k in range(1, NX))
    product = jnp.concatenate([share] + [shift(share, "x", -k) for k in range(1, NX)], 0)

    prod = [product] + [shift(product, "y", k) for k in range(1, NY)]
    b_col = [b[0]] + [shift(b[k], "y", k) for k in range(1, NY)]

    gram = gram_of(product)
    keep = jnp.where(c == 0, gram[:768], gram[768:])
    give = jnp.where(c == 0, gram[768:], gram[:768])
    keep = keep + shift(give, "c", 1)
    parts = lax.all_to_all(keep.reshape(NY * NZ, 24, 128), ("y", "z"), 0, 0, tiled=True)
    keep = spread(parts.sum(0), ("y", "z"), NY * NZ).reshape(768, 128)
    blocks = pair(c, keep, shift(keep, "c", 1)).reshape(1536, 128)
    w = factor_inverse(blocks)

    p_own, p_factor, right = right_of(place, w, prod, b_col)
    right = right[0] + shift(right[1], "c", 1)
    pieces = lax.all_to_all(right.reshape(NZ, PIECE, RANK), "z", 0, 0, tiled=True)
    r_mine = pieces.sum(0)

    r_own, r_other = gather_rows(r_mine.astype(BF16))
    momentum_next = update_of(place, p_own, r_own, r_other, momentum, grad)

    power = jnp.sum(r_mine * r_mine, axis=0, keepdims=True)
    power = power + shift(power, "c", 1)
    power = power + sum(shift(power, "x", k) for k in range(1, NX))
    power = power + sum(shift(power, "y", k) for k in range(1, NY))
    power = spread(power, "z", NZ).sum(0)
    q_next = r_mine * lax.rsqrt(power / COLS + 1e-06)
    return p_factor, q_next, momentum_next


def solution(mesh):
    inner = Mesh(np.asarray(mesh.devices).reshape(NY, NZ, NC, NX), ("y", "z", "c", "x"))
    row, col = ("y", "z", "c"), "x"
    in_specs = (P(row, col), P(row, col), P((col,) + row, None))
    out_specs = (P(row + (col,), None), P((col,) + row, None), P(row, col))
    return jax.shard_map(body, mesh=inner, in_specs=in_specs, out_specs=out_specs, check_vma=False)
```

```python
import jax
import jax.numpy as jnp
import numpy as np
from jax import lax
from jax.experimental import pallas as pl
from jax.experimental.pallas import tpu as pltpu
from jax.sharding import Mesh, PartitionSpec as P

ROWS = 28672
COLS = 8192
RANK = 512
DECAY = 0.05

NY, NZ, NC, NX = 4, 8, 2, 4
ROW_LOCAL = ROWS // (NY * NZ * NC)
SHARE = ROW_LOCAL // NX
BLOCK = 512
HALF = 768
PIECE = 32
F32, BF16 = jnp.float32, jnp.bfloat16
SIZES = {"y": NY, "z": NZ, "c": NC, "x": NX}
VMEM = pl.BlockSpec(memory_space=pltpu.VMEM)
SMEM = pl.BlockSpec(memory_space=pltpu.SMEM)
PARAMS = pltpu.CompilerParams(vmem_limit_bytes=48 * 1024 * 1024)
HIGH = lax.Precision.HIGHEST


def shift(x, axis, k):
    n = SIZES[axis]
    return lax.ppermute(x, axis, [(i, (i + k) % n) for i in range(n)])


def spread(x, axes, n):
    full = jnp.broadcast_to(x[None], (n,) + x.shape)
    return lax.all_to_all(full, axes, 0, 0, tiled=True)


def prep_kernel(place, m_ref, g_ref, b_ref):
    for k in range(NX):
        start = pl.multiple_of(lax.rem(place[0] + k, NX) * SHARE, SHARE)
        mixed = m_ref[pl.ds(start, SHARE), :] + g_ref[pl.ds(start, SHARE), :].astype(F32)
        b_ref[0, pl.ds(k * SHARE, SHARE), :] = mixed.astype(BF16)


def prep(place, momentum, grad):
    spec = pl.BlockSpec((ROW_LOCAL, BLOCK), lambda k, s: (0, lax.rem(s[1] + k, NY)))
    return pl.pallas_call(
        prep_kernel,
        grid_spec=pltpu.PrefetchScalarGridSpec(
            num_scalar_prefetch=1,
            grid=(NY,),
            in_specs=[spec, spec],
            out_specs=pl.BlockSpec((1, ROW_LOCAL, BLOCK), lambda k, s: (k, 0, 0)),
        ),
        out_shape=jax.ShapeDtypeStruct((NY, ROW_LOCAL, BLOCK), BF16),
        compiler_params=PARAMS,
        cost_estimate=pl.CostEstimate(flops=10**6, bytes_accessed=16 * 2**20, transcendentals=0),
    )(place, momentum, grad)


def weave(place, mine, other, whole):
    c = place[2]
    for z in range(NZ):
        at = pl.multiple_of(z * 2 * PIECE + c * PIECE, PIECE)
        whole[pl.ds(at, PIECE), :] = mine[pl.ds(z * PIECE, PIECE), :]
        at = pl.multiple_of(z * 2 * PIECE + (1 - c) * PIECE, PIECE)
        whole[pl.ds(at, PIECE), :] = other[pl.ds(z * PIECE, PIECE), :]


def product_kernel(place, b_ref, *refs):
    mine, other, out, whole = refs[:NY], refs[NY : 2 * NY], refs[2 * NY], refs[2 * NY + 1]
    for k in range(NY):
        weave(place, mine[k], other[k], whole.at[k])
    total = jnp.dot(b_ref[0], whole[0], preferred_element_type=F32)
    for k in range(1, NY):
        total += jnp.dot(b_ref[k], whole[k], preferred_element_type=F32)
    out[...] = total


def product_of(place, b, mine, other):
    return pl.pallas_call(
        product_kernel,
        in_specs=[SMEM] + [VMEM] * (1 + 2 * NY),
        out_specs=VMEM,
        out_shape=jax.ShapeDtypeStruct((ROW_LOCAL, RANK), F32),
        scratch_shapes=[pltpu.VMEM((NY, BLOCK, RANK), BF16)],
        compiler_params=PARAMS,
    )(place, b, *mine, *other)


def gram_kernel(place, *refs):
    shares, keep, give, whole = refs[:NX], refs[NX], refs[NX + 1], refs[NX + 2]
    p = jnp.concatenate([v[...] for v in shares], 0)
    left, right = p[:, :256], p[:, 256:]
    for i, (a, b) in enumerate(((left, left), (right, left), (right, right))):
        g = lax.dot_general(a, b, (((0,), (0,)), ((), ())), precision=HIGH, preferred_element_type=F32)
        whole[pl.ds(i * 512, 256), :] = g[:, :128]
        whole[pl.ds(i * 512 + 256, 256), :] = g[:, 128:]
    keep[...] = whole[pl.ds(pl.multiple_of(place[2] * HALF, HALF), HALF), :]
    give[...] = whole[pl.ds(pl.multiple_of((1 - place[2]) * HALF, HALF), HALF), :]


def gram_of(place, shares):
    half = jax.ShapeDtypeStruct((HALF, 128), F32)
    return pl.pallas_call(
        gram_kernel,
        in_specs=[SMEM] + [VMEM] * NX,
        out_specs=[VMEM] * 2,
        out_shape=[half, half],
        scratch_shapes=[pltpu.VMEM((2 * HALF, 128), F32)],
        compiler_params=PARAMS,
    )(place, *shares)


def sum_spread_kernel(parts, out):
    total = jnp.sum(parts[...], axis=0)
    for i in range(out.shape[0]):
        out[i] = total


def sum_spread(parts):
    return pl.pallas_call(
        sum_spread_kernel,
        in_specs=[VMEM],
        out_specs=VMEM,
        out_shape=jax.ShapeDtypeStruct(parts.shape, F32),
        compiler_params=PARAMS,
    )(parts)


def row_of(v, j):
    return jnp.broadcast_to(v[j : j + 1, :], v.shape)


def diag_inverse(m_ref, w_ref):
    n = m_ref.shape[0]
    lane = lax.broadcasted_iota(jnp.int32, (8, n), 1)
    sub = lax.broadcasted_iota(jnp.int32, (8, n), 0)
    groups = n // 8
    for p in range(groups):
        raw = [m_ref[8 * g : 8 * g + 8, :] for g in range(p, groups)]
        cols = [[jnp.broadcast_to(r[:, 8 * p + k : 8 * p + k + 1], (8, n)) for k in range(8)] for r in raw]
        pivot = list(cols[0])
        panel = (lane >= 8 * p) & (lane < 8 * p + 8)
        rows = jnp.where(panel, jnp.where(lane - 8 * p == sub, 1.0, 0.0), raw[0])
        done = jnp.zeros((8, n), F32)
        for j in range(8):
            d = row_of(pivot[j], j)
            inv = 1.0 / d
            at = sub == j
            row = row_of(rows, j)
            done = jnp.where(at, row * lax.rsqrt(d), done)
            row = row * inv
            rows = jnp.where(at, row, rows - pivot[j] * row)
            for k in range(j + 1, 8):
                t = row_of(pivot[k], j) * inv
                pivot[k] = jnp.where(at, t, pivot[k] - pivot[j] * t)
        w_ref[8 * p : 8 * p + 8, :] = jnp.where(lane < 8 * p + 8, done, 0.0)
        z = [row_of(rows, k) for k in range(8)]
        for g in range(p + 1, groups):
            v = jnp.where(panel, 0.0, raw[g - p])
            for k in range(8):
                v = v - cols[g - p][k] * z[k]
            m_ref[8 * g : 8 * g + 8, :] = v


def fdot(a, b, tb=False):
    dims = (((1,), (1 if tb else 0,)), ((), ()))
    return lax.dot_general(a, b, dims, precision=HIGH, preferred_element_type=F32)


def factor_kernel(place, mine, other, w, a, m, d):
    c = place[2]
    for h in range(NC):
        part = jnp.where(c == h, mine[...], other[...])
        for q in range(3):
            at = h * 3 + q
            i, j = ((0, 0), (1, 0), (1, 1))[at // 2]
            cols = j * 256 + at % 2 * 128
            a[i * 256 : i * 256 + 256, cols : cols + 128] = part[q * 256 : q * 256 + 256]
    w[...] = jnp.zeros((RANK, RANK), F32)
    for k in range(RANK // 128):
        o, e = k * 128, k * 128 + 128
        m[...] = a[o:e, o:e]
        diag_inverse(m, d)
        wd = d[...]
        w[o:e, o:e] = wd
        if k:
            w[o:e, 0:o] = fdot(wd, w[o:e, 0:o])
        if e < RANK:
            low = fdot(a[e:, o:e], wd, tb=True)
            for at in range(0, RANK - e, 128):
                cols = slice(e + at, e + at + 128)
                a[e + at :, cols] = a[e + at :, cols] - fdot(low[at:], low[at : at + 128], tb=True)
            w[e:, 0:e] = w[e:, 0:e] - fdot(low, w[o:e, 0:e])


def factor_inverse(place, mine, other):
    return pl.pallas_call(
        factor_kernel,
        in_specs=[SMEM, VMEM, VMEM],
        out_specs=VMEM,
        out_shape=jax.ShapeDtypeStruct((RANK, RANK), F32),
        scratch_shapes=[pltpu.VMEM((RANK, RANK), F32)] + [pltpu.VMEM((128, 128), F32)] * 2,
        compiler_params=PARAMS,
        cost_estimate=pl.CostEstimate(flops=10**10, bytes_accessed=2 * 2**20, transcendentals=0),
    )(place, mine, other)


def right_kernel(place, w_ref, *refs):
    near, far, b = refs[:NX], refs[NX : 2 * NX], refs[2 * NX : 2 * NX + NY]
    p_own, p_factor, keep, give, total = refs[2 * NX + NY :]
    w_top, w_low = w_ref[:256, :256], w_ref[256:, :]
    for i in range(NX):
        rows = slice(i * SHARE, (i + 1) * SHARE)
        prod = jnp.concatenate([near[i][...], far[i][...]], 0)
        p = jnp.concatenate([fdot(prod[:, :256], w_top, tb=True), fdot(prod, w_low, tb=True)], 1)
        half = p.astype(BF16)
        if i == 0:
            p_factor[...] = p[:SHARE] * jnp.sqrt(F32(ROWS))
        p_own[rows, :] = half[:SHARE]
        cols = jnp.concatenate([v[rows, :] for v in b], 0)
        part = lax.dot_general(cols, half, (((0,), (0,)), ((), ())), preferred_element_type=F32)
        if i == 0:
            total[...] = part
        else:
            total[...] += part
    c = place[2]
    for z in range(NZ):
        at = pl.multiple_of(z * 2 * PIECE + c * PIECE, PIECE)
        keep[pl.ds(z * PIECE, PIECE), :] = total[pl.ds(at, PIECE), :]
        at = pl.multiple_of(z * 2 * PIECE + (1 - c) * PIECE, PIECE)
        give[pl.ds(z * PIECE, PIECE), :] = total[pl.ds(at, PIECE), :]


def right_of(place, w, near, far, b):
    half = jax.ShapeDtypeStruct((NZ * PIECE, RANK), F32)
    return pl.pallas_call(
        right_kernel,
        in_specs=[SMEM] + [VMEM] * (1 + 2 * NX + NY),
        out_specs=[VMEM] * 4,
        out_shape=[
            jax.ShapeDtypeStruct((ROW_LOCAL, RANK), BF16),
            jax.ShapeDtypeStruct((SHARE, RANK), F32),
            half,
            half,
        ],
        scratch_shapes=[pltpu.VMEM((BLOCK, RANK), F32)],
        compiler_params=PARAMS,
    )(place, w, *near, *far, *b)


def rows_kernel(pieces, r_mine, out):
    r = jnp.sum(pieces[...], axis=0)
    r_mine[...] = r
    half = r.astype(BF16)
    power = jnp.sum(r * r, axis=0, keepdims=True)
    high = power.astype(BF16)
    rest = power - high.astype(F32)
    mid = rest.astype(BF16)
    low = (rest - mid.astype(F32)).astype(BF16)
    sub = lax.broadcasted_iota(jnp.int32, (16, RANK), 0)
    spread_to = lambda v: jnp.broadcast_to(v.astype(F32), (16, RANK))
    tail = jnp.where(sub == 0, spread_to(high), jnp.where(sub == 1, spread_to(mid), spread_to(low)))
    tail = jnp.where(sub < 3, tail, 0.0).astype(BF16)
    for i in range(NZ):
        out[i, :PIECE, :] = half
        out[i, PIECE:, :] = tail


def rows_of(pieces):
    return pl.pallas_call(
        rows_kernel,
        in_specs=[VMEM],
        out_specs=[VMEM] * 2,
        out_shape=[
            jax.ShapeDtypeStruct((PIECE, RANK), F32),
            jax.ShapeDtypeStruct((NZ, PIECE + 16, RANK), BF16),
        ],
        compiler_params=PARAMS,
    )(pieces)


def update_kernel(place, p_ref, *refs):
    mine, other = refs[:NY], refs[NY : 2 * NY]
    m_ref, g_ref, out, whole = refs[2 * NY :]
    step = pl.program_id(0)
    for k in range(NY):

        @pl.when(step == k)
        def _():
            weave(place, mine[k], other[k], whole)

    update = lax.dot_general(
        p_ref[...], whole[...], (((1,), (1,)), ((), ())), preferred_element_type=F32
    )
    for k in range(NX):
        start = pl.multiple_of(lax.rem(place[0] + k, NX) * SHARE, SHARE)
        mixed = m_ref[pl.ds(start, SHARE), :] + g_ref[pl.ds(start, SHARE), :].astype(F32)
        out[pl.ds(start, SHARE), :] = mixed - DECAY * update[k * SHARE : (k + 1) * SHARE]


def update_of(place, p_own, mine, other, momentum, grad):
    spec = pl.BlockSpec((ROW_LOCAL, BLOCK), lambda k, s: (0, lax.rem(s[1] + k, NY)))
    return pl.pallas_call(
        update_kernel,
        grid_spec=pltpu.PrefetchScalarGridSpec(
            num_scalar_prefetch=1,
            grid=(NY,),
            in_specs=[VMEM] * (1 + 2 * NY) + [spec, spec],
            out_specs=spec,
            scratch_shapes=[pltpu.VMEM((BLOCK, RANK), BF16)],
        ),
        out_shape=jax.ShapeDtypeStruct((ROW_LOCAL, NY * BLOCK), F32),
        compiler_params=PARAMS,
    )(place, p_own, *mine, *other, momentum, grad)


def gather_cols(own):
    mine = [own] + [shift(own, "y", -k) for k in range(1, NY)]
    other = [shift(v, "c", 1) for v in mine]
    return mine, other


def body(momentum, grad, q_basis):
    x, y, c = lax.axis_index("x"), lax.axis_index("y"), lax.axis_index("c")
    place = jnp.stack([x, y, c]).astype(jnp.int32)

    q_own = spread(q_basis.astype(BF16), "z", NZ).reshape(NZ * PIECE, RANK)
    q_mine, q_other = gather_cols(q_own)
    b = prep(place, momentum, grad)
    partial = product_of(place, b, q_mine, q_other).reshape(NX, SHARE, RANK)

    share = partial[0] + sum(shift(partial[k], "x", k) for k in range(1, NX))
    near = [share] + [shift(share, "x", -k) for k in range(1, NX)]
    b_col = [b[0]] + [shift(b[k], "y", k) for k in range(1, NY)]
    rest = jnp.concatenate([shift(share, "y", k) for k in range(1, NY)], 0)
    far = [rest] + [shift(rest, "x", -k) for k in range(1, NX)]

    keep, give = gram_of(place, near)
    keep = keep + shift(give, "c", 1)
    parts = lax.all_to_all(keep.reshape(NY * NZ, 24, 128), ("y", "z"), 0, 0, tiled=True)
    mine = lax.all_to_all(sum_spread(parts), ("y", "z"), 0, 0, tiled=True).reshape(HALF, 128)
    w = factor_inverse(place, mine, shift(mine, "c", 1))

    p_own, p_factor, keep, give = right_of(place, w, near, far, b_col)
    right = keep + shift(give, "c", 1)
    pieces = lax.all_to_all(right.reshape(NZ, PIECE, RANK), "z", 0, 0, tiled=True)
    r_mine, rows = rows_of(pieces)
    rows = lax.all_to_all(rows, "z", 0, 0, tiled=True)
    r_own, r_other = gather_cols(rows[:, :PIECE].reshape(NZ * PIECE, RANK))
    momentum_next = update_of(place, p_own, r_own, r_other, momentum, grad)

    power = jnp.sum(rows[:, PIECE : PIECE + 3].astype(F32), axis=(0, 1))[None]
    power = power + shift(power, "c", 1)
    power = power + sum(shift(power, "x", k) for k in range(1, NX))
    power = power + sum(shift(power, "y", k) for k in range(1, NY))
    q_next = r_mine * lax.rsqrt(power / COLS + 1e-06)
    return p_factor, q_next, momentum_next


def solution(mesh):
    inner = Mesh(np.asarray(mesh.devices).reshape(NY, NZ, NC, NX), ("y", "z", "c", "x"))
    row, col = ("y", "z", "c"), "x"
    in_specs = (P(row, col), P(row, col), P((col,) + row, None))
    out_specs = (P(row + (col,), None), P((col,) + row, None), P(row, col))
    return jax.shard_map(body, mesh=inner, in_specs=in_specs, out_specs=out_specs, check_vma=False)
```

```python
import functools

import jax
import jax.numpy as jnp
import numpy as np
from jax import lax
from jax.experimental import pallas as pl
from jax.experimental.pallas import tpu as pltpu
from jax.sharding import Mesh, PartitionSpec as P

ROWS = 28672
COLS = 8192
RANK = 512
DECAY = 0.05

NY, NZ, NC, NX = 4, 8, 2, 4
ROW_LOCAL = ROWS // (NY * NZ * NC)
SHARE = ROW_LOCAL // NX
BLOCK = 512
HALF = 768
TAIL = 16
PIECE = 32
F32, BF16 = jnp.float32, jnp.bfloat16
SIZES = {"y": NY, "z": NZ, "c": NC, "x": NX}
VMEM = pl.BlockSpec(memory_space=pltpu.VMEM)
SMEM = pl.BlockSpec(memory_space=pltpu.SMEM)
PARAMS = pltpu.CompilerParams(vmem_limit_bytes=20 * 1024 * 1024)
HIGH = lax.Precision.HIGHEST


def shift(x, axis, k):
    n = SIZES[axis]
    return lax.ppermute(x, axis, [(i, (i + k) % n) for i in range(n)])


def spread(x, axes, n):
    full = jnp.broadcast_to(x[None], (n,) + x.shape)
    return lax.all_to_all(full, axes, 0, 0, tiled=True)


def after(values, *first):
    n = len(values)
    return pl.pallas_call(
        lambda *refs: None,
        in_specs=[VMEM] * (n + len(first)),
        out_specs=[VMEM] * n,
        out_shape=[jax.ShapeDtypeStruct(v.shape, v.dtype) for v in values],
        input_output_aliases={i: i for i in range(n)},
        compiler_params=PARAMS,
    )(*values, *first)


def prep_kernel(place, m_ref, g_ref, b_ref):
    for k in range(NX):
        start = pl.multiple_of(lax.rem(place[0] + k, NX) * SHARE, SHARE)
        mixed = m_ref[pl.ds(start, SHARE), :] + g_ref[pl.ds(start, SHARE), :].astype(F32)
        b_ref[0, pl.ds(k * SHARE, SHARE), :] = mixed.astype(BF16)


def prep(place, momentum, grad):
    spec = pl.BlockSpec((ROW_LOCAL, BLOCK), lambda k, s: (0, lax.rem(s[1] + k, NY)))
    return pl.pallas_call(
        prep_kernel,
        grid_spec=pltpu.PrefetchScalarGridSpec(
            num_scalar_prefetch=1,
            grid=(NY,),
            in_specs=[spec, spec],
            out_specs=pl.BlockSpec((1, ROW_LOCAL, BLOCK), lambda k, s: (k, 0, 0)),
        ),
        out_shape=jax.ShapeDtypeStruct((NY, ROW_LOCAL, BLOCK), BF16),
        compiler_params=PARAMS,
        cost_estimate=pl.CostEstimate(flops=10**6, bytes_accessed=16 * 2**20, transcendentals=0),
    )(place, momentum, grad)


def weave(place, mine, other, whole):
    c = place[2]
    for z in range(NZ):
        at = pl.multiple_of(z * 2 * PIECE + c * PIECE, PIECE)
        whole[pl.ds(at, PIECE), :] = mine[pl.ds(z * PIECE, PIECE), :]
        at = pl.multiple_of(z * 2 * PIECE + (1 - c) * PIECE, PIECE)
        whole[pl.ds(at, PIECE), :] = other[pl.ds(z * PIECE, PIECE), :]


def product_kernel(place, b_ref, *refs):
    mine, other, out, whole = refs[:NY], refs[NY : 2 * NY], refs[2 * NY], refs[2 * NY + 1]
    for k in range(NY):
        weave(place, mine[k], other[k], whole.at[k])
    total = jnp.dot(b_ref[0], whole[0], preferred_element_type=F32)
    for k in range(1, NY):
        total += jnp.dot(b_ref[k], whole[k], preferred_element_type=F32)
    out[...] = total


def product_of(place, b, mine, other):
    return pl.pallas_call(
        product_kernel,
        in_specs=[SMEM] + [VMEM] * (1 + 2 * NY),
        out_specs=VMEM,
        out_shape=jax.ShapeDtypeStruct((ROW_LOCAL, RANK), F32),
        scratch_shapes=[pltpu.VMEM((NY, BLOCK, RANK), BF16)],
        compiler_params=PARAMS,
    )(place, b, *mine, *other)


def gram_kernel(place, *refs):
    shares, (keep, give, whole) = refs[:NX], refs[-3:]
    p = jnp.concatenate([v[...] for v in shares], 0)
    left, right = p[:, :256], p[:, 256:]
    for i, (a, b) in enumerate(((left, left), (right, left), (right, right))):
        g = lax.dot_general(a, b, (((0,), (0,)), ((), ())), precision=HIGH, preferred_element_type=F32)
        whole[pl.ds(i * 512, 256), :] = g[:, :128]
        whole[pl.ds(i * 512 + 256, 256), :] = g[:, 128:]
    keep[...] = whole[pl.ds(pl.multiple_of(place[2] * HALF, HALF), HALF), :]
    give[...] = whole[pl.ds(pl.multiple_of((1 - place[2]) * HALF, HALF), HALF), :]


def gram_of(place, shares, first):
    half = jax.ShapeDtypeStruct((HALF, 128), F32)
    return pl.pallas_call(
        gram_kernel,
        in_specs=[SMEM] + [VMEM] * (NX + len(first)),
        out_specs=[VMEM] * 2,
        out_shape=[half, half],
        scratch_shapes=[pltpu.VMEM((2 * HALF, 128), F32)],
        compiler_params=PARAMS,
    )(place, *shares, *first)


def add_kernel(*refs):
    refs[-1][...] = refs[0][...] + refs[1][...]


def add_after(a, b, *first):
    return pl.pallas_call(
        add_kernel,
        in_specs=[VMEM] * (2 + len(first)),
        out_specs=VMEM,
        out_shape=jax.ShapeDtypeStruct(a.shape, a.dtype),
        compiler_params=PARAMS,
    )(a, b, *first)


def sum_spread_kernel(parts, out):
    total = jnp.sum(parts[...], axis=0)
    for i in range(out.shape[0]):
        out[i] = total


def sum_spread(parts):
    return pl.pallas_call(
        sum_spread_kernel,
        in_specs=[VMEM],
        out_specs=VMEM,
        out_shape=jax.ShapeDtypeStruct(parts.shape, F32),
        compiler_params=PARAMS,
    )(parts)


def row_of(v, j):
    return jnp.broadcast_to(v[j : j + 1, :], v.shape)


def diag_inverse(m_ref, w_ref):
    n = m_ref.shape[0]
    lane = lax.broadcasted_iota(jnp.int32, (8, n), 1)
    sub = lax.broadcasted_iota(jnp.int32, (8, n), 0)
    groups = n // 8
    for p in range(groups):
        raw = [m_ref[8 * g : 8 * g + 8, :] for g in range(p, groups)]
        cols = [[jnp.broadcast_to(r[:, 8 * p + k : 8 * p + k + 1], (8, n)) for k in range(8)] for r in raw]
        pivot = list(cols[0])
        panel = (lane >= 8 * p) & (lane < 8 * p + 8)
        rows = jnp.where(panel, jnp.where(lane - 8 * p == sub, 1.0, 0.0), raw[0])
        done = jnp.zeros((8, n), F32)
        for j in range(8):
            d = row_of(pivot[j], j)
            inv = 1.0 / d
            at = sub == j
            row = row_of(rows, j)
            done = jnp.where(at, row * lax.rsqrt(d), done)
            row = row * inv
            rows = jnp.where(at, row, rows - pivot[j] * row)
            for k in range(j + 1, 8):
                t = row_of(pivot[k], j) * inv
                pivot[k] = jnp.where(at, t, pivot[k] - pivot[j] * t)
        w_ref[8 * p : 8 * p + 8, :] = jnp.where(lane < 8 * p + 8, done, 0.0)
        z = [row_of(rows, k) for k in range(8)]
        for g in range(p + 1, groups):
            v = jnp.where(panel, 0.0, raw[g - p])
            for k in range(8):
                v = v - cols[g - p][k] * z[k]
            m_ref[8 * g : 8 * g + 8, :] = v


def fdot(a, b, tb=False):
    dims = (((1,), (1 if tb else 0,)), ((), ()))
    return lax.dot_general(a, b, dims, precision=HIGH, preferred_element_type=F32)


def factor_kernel(place, mine, other, w, a, m, d):
    c = place[2]
    for h in range(NC):
        part = jnp.where(c == h, mine[...], other[...])
        for q in range(3):
            at = h * 3 + q
            i, j = ((0, 0), (1, 0), (1, 1))[at // 2]
            cols = j * 256 + at % 2 * 128
            a[i * 256 : i * 256 + 256, cols : cols + 128] = part[q * 256 : q * 256 + 256]
    w[...] = jnp.zeros((RANK, RANK), F32)
    for k in range(RANK // 128):
        o, e = k * 128, k * 128 + 128
        m[...] = a[o:e, o:e]
        diag_inverse(m, d)
        wd = d[...]
        w[o:e, o:e] = wd
        if k:
            w[o:e, 0:o] = fdot(wd, w[o:e, 0:o])
        if e < RANK:
            low = fdot(a[e:, o:e], wd, tb=True)
            for at in range(0, RANK - e, 128):
                cols = slice(e + at, e + at + 128)
                a[e + at :, cols] = a[e + at :, cols] - fdot(low[at:], low[at : at + 128], tb=True)
            w[e:, 0:e] = w[e:, 0:e] - fdot(low, w[o:e, 0:e])


def factor_inverse(place, mine, other):
    return pl.pallas_call(
        factor_kernel,
        in_specs=[SMEM, VMEM, VMEM],
        out_specs=VMEM,
        out_shape=jax.ShapeDtypeStruct((RANK, RANK), F32),
        scratch_shapes=[pltpu.VMEM((RANK, RANK), F32)] + [pltpu.VMEM((128, 128), F32)] * 2,
        compiler_params=PARAMS,
        cost_estimate=pl.CostEstimate(flops=5 * 10**9, bytes_accessed=2 * 2**20, transcendentals=0),
    )(place, mine, other)


def right_kernel(place, w_ref, *refs):
    near, far, b = refs[:NX], refs[NX : 2 * NX], refs[2 * NX : 2 * NX + NY]
    p_own, p_factor, keep, give, total = refs[2 * NX + NY :]
    w_top, w_low = w_ref[:256, :256], w_ref[256:, :]
    for i in range(NX):
        rows = slice(i * SHARE, (i + 1) * SHARE)
        prod = jnp.concatenate([near[i][...], far[i][...]], 0)
        p = jnp.concatenate([fdot(prod[:, :256], w_top, tb=True), fdot(prod, w_low, tb=True)], 1)
        half = p.astype(BF16)
        if i == 0:
            p_factor[...] = p[:SHARE] * jnp.sqrt(F32(ROWS))
        p_own[rows, :] = half[:SHARE]
        cols = jnp.concatenate([v[rows, :] for v in b], 0)
        part = lax.dot_general(cols, half, (((0,), (0,)), ((), ())), preferred_element_type=F32)
        if i == 0:
            total[...] = part
        else:
            total[...] += part
    c = place[2]
    for z in range(NZ):
        at = pl.multiple_of(z * 2 * PIECE + c * PIECE, PIECE)
        keep[pl.ds(z * PIECE, PIECE), :] = total[pl.ds(at, PIECE), :]
        at = pl.multiple_of(z * 2 * PIECE + (1 - c) * PIECE, PIECE)
        give[pl.ds(z * PIECE, PIECE), :] = total[pl.ds(at, PIECE), :]


def right_of(place, w, near, far, b):
    half = jax.ShapeDtypeStruct((NZ * PIECE, RANK), F32)
    return pl.pallas_call(
        right_kernel,
        in_specs=[SMEM] + [VMEM] * (1 + 2 * NX + NY),
        out_specs=[VMEM] * 4,
        out_shape=[
            jax.ShapeDtypeStruct((ROW_LOCAL, RANK), BF16),
            jax.ShapeDtypeStruct((SHARE, RANK), F32),
            half,
            half,
        ],
        scratch_shapes=[pltpu.VMEM((BLOCK, RANK), F32)],
        compiler_params=PARAMS,
    )(place, w, *near, *far, *b)


def tail_of(power):
    high = power.astype(BF16)
    rest = power - high.astype(F32)
    mid = rest.astype(BF16)
    low = (rest - mid.astype(F32)).astype(BF16)
    sub = lax.broadcasted_iota(jnp.int32, (TAIL, RANK), 0)
    high, mid, low = (jnp.broadcast_to(v.astype(F32), (TAIL, RANK)) for v in (high, mid, low))
    tail = jnp.where(sub == 0, high, jnp.where(sub == 1, mid, low))
    return jnp.where(sub < 3, tail, 0.0).astype(BF16)


def rows_kernel(pieces, r_mine, out):
    r = jnp.sum(pieces[...], axis=0)
    r_mine[...] = r
    half = r.astype(BF16)
    tail = tail_of(jnp.sum(r * r, axis=0, keepdims=True))
    for i in range(NZ):
        out[i, :PIECE, :] = half
        out[i, PIECE:, :] = tail


def rows_of(pieces):
    return pl.pallas_call(
        rows_kernel,
        in_specs=[VMEM],
        out_specs=[VMEM] * 2,
        out_shape=[
            jax.ShapeDtypeStruct((PIECE, RANK), F32),
            jax.ShapeDtypeStruct((NZ, PIECE + TAIL, RANK), BF16),
        ],
        compiler_params=PARAMS,
    )(pieces)


def pack_kernel(rows, out):
    power = jnp.zeros((1, RANK), F32)
    for z in range(NZ):
        out[pl.ds(z * PIECE, PIECE), :] = rows[z, :PIECE, :]
        power += jnp.sum(rows[z, PIECE:, :].astype(F32), axis=0, keepdims=True)
    out[pl.ds(NZ * PIECE, TAIL), :] = tail_of(power)


def pack(rows):
    return pl.pallas_call(
        pack_kernel,
        in_specs=[VMEM],
        out_specs=VMEM,
        out_shape=jax.ShapeDtypeStruct((NZ * PIECE + TAIL, RANK), BF16),
        compiler_params=PARAMS,
    )(rows)


def power_kernel(*refs):
    power = jnp.zeros((1, RANK), F32)
    for v in refs[:-1]:
        power += jnp.sum(v[pl.ds(NZ * PIECE, TAIL), :].astype(F32), axis=0, keepdims=True)
    refs[-1][...] = power


def power_of(chunks):
    return pl.pallas_call(
        power_kernel,
        in_specs=[VMEM] * len(chunks),
        out_specs=VMEM,
        out_shape=jax.ShapeDtypeStruct((1, RANK), F32),
        compiler_params=PARAMS,
    )(*chunks)


def update_kernel(n, place, p_ref, *refs):
    mine, other = refs[:n], refs[n : 2 * n]
    m_ref, g_ref, out, whole = refs[2 * n], refs[2 * n + 1], refs[-2], refs[-1]
    for k in range(n):

        @pl.when(pl.program_id(0) == k)
        def _():
            weave(place, mine[k], other[k], whole)

    update = lax.dot_general(
        p_ref[...], whole[...], (((1,), (1,)), ((), ())), preferred_element_type=F32
    )
    for k in range(NX):
        start = pl.multiple_of(lax.rem(place[0] + k, NX) * SHARE, SHARE)
        mixed = m_ref[pl.ds(start, SHARE), :] + g_ref[pl.ds(start, SHARE), :].astype(F32)
        out[pl.ds(start, SHARE), :] = mixed - DECAY * update[k * SHARE : (k + 1) * SHARE]


def update_of(place, p_own, mine, other, momentum, grad, first, step, before=None):
    n = len(mine)
    spec = pl.BlockSpec((ROW_LOCAL, BLOCK), lambda k, s: (0, lax.rem(s[1] + first + step * k, NY)))
    more = [] if before is None else [before]
    return pl.pallas_call(
        functools.partial(update_kernel, n),
        grid_spec=pltpu.PrefetchScalarGridSpec(
            num_scalar_prefetch=1,
            grid=(n,),
            in_specs=[VMEM] * (1 + 2 * n) + [spec, spec] + [pl.BlockSpec(memory_space=pl.ANY)] * len(more),
            out_specs=spec,
            scratch_shapes=[pltpu.VMEM((BLOCK, RANK), BF16)],
        ),
        out_shape=jax.ShapeDtypeStruct((ROW_LOCAL, NY * BLOCK), F32),
        input_output_aliases={4 + 2 * n: 0} if more else {},
        compiler_params=PARAMS,
        cost_estimate=pl.CostEstimate(flops=n * 2**28, bytes_accessed=n * 3 * 2**20, transcendentals=0),
    )(place, p_own, *mine, *other, momentum, grad, *more)


def body(momentum, grad, q_basis):
    x, y, c = lax.axis_index("x"), lax.axis_index("y"), lax.axis_index("c")
    place = jnp.stack([x, y, c]).astype(jnp.int32)

    q_own = spread(q_basis.astype(BF16), "z", NZ).reshape(NZ * PIECE, RANK)
    b = prep(place, momentum, grad)
    q_mine = [shift(q_own, "y", -k) for k in range(1, NY)]
    q_mine = [q_own, *after(q_mine, b)]
    q_other = [shift(v, "c", 1) for v in q_mine]
    partial = product_of(place, b, q_mine, q_other).reshape(NX, SHARE, RANK)

    share = partial[0] + sum(shift(partial[k], "x", k) for k in range(1, NX))
    near = [share] + [shift(share, "x", -k) for k in range(1, NX)]
    b_col = [b[0]] + [shift(b[k], "y", k) for k in range(1, NY)]
    rest = jnp.concatenate([shift(share, "y", k) for k in range(1, NY)], 0)
    far = [rest] + [shift(rest, "x", -k) for k in range(1, NX)]

    keep, give = gram_of(place, near, b_col[1:])
    keep = add_after(keep, shift(give, "c", 1), rest)
    parts = lax.all_to_all(keep.reshape(NY * NZ, 24, 128), ("y", "z"), 0, 0, tiled=True)
    mine = lax.all_to_all(sum_spread(parts), ("y", "z"), 0, 0, tiled=True).reshape(HALF, 128)
    w = factor_inverse(place, mine, shift(mine, "c", 1))

    p_own, p_factor, keep, give = right_of(place, w, near, far, b_col)
    right = keep + shift(give, "c", 1)
    pieces = lax.all_to_all(right.reshape(NZ, PIECE, RANK), "z", 0, 0, tiled=True)
    r_mine, rows = rows_of(pieces)
    r_own = pack(lax.all_to_all(rows, "z", 0, 0, tiled=True))
    r_mine_cols = [r_own] + [shift(r_own, "y", -k) for k in range(1, NY)]
    r_other = [shift(v, "c", 1) for v in r_mine_cols]

    given = (momentum, grad)
    out = update_of(place, p_own, r_mine_cols[:1], r_other[:1], *given, 0, 1)
    out = update_of(place, p_own, r_mine_cols[1::2], r_other[1::2], *given, 1, 2, out)
    out = update_of(place, p_own, r_mine_cols[2:3], r_other[2:3], *given, 2, 1, out)

    power = power_of(r_mine_cols + r_other)
    power = power + sum(shift(power, "x", k) for k in range(1, NX))
    q_next = r_mine * lax.rsqrt(power / COLS + 1e-06)
    return p_factor, q_next, out


def solution(mesh):
    inner = Mesh(np.asarray(mesh.devices).reshape(NY, NZ, NC, NX), ("y", "z", "c", "x"))
    row, col = ("y", "z", "c"), "x"
    in_specs = (P(row, col), P(row, col), P((col,) + row, None))
    out_specs = (P(row + (col,), None), P((col,) + row, None), P(row, col))
    return jax.shard_map(body, mesh=inner, in_specs=in_specs, out_specs=out_specs, check_vma=False)
```

```python
import functools

import jax
import jax.numpy as jnp
import numpy as np
from jax import lax
from jax.experimental import pallas as pl
from jax.experimental.pallas import tpu as pltpu
from jax.sharding import Mesh, PartitionSpec as P

ROWS = 28672
COLS = 8192
RANK = 512
DECAY = 0.05

NY, NZ, NC, NX = 4, 8, 2, 4
ROW_LOCAL = ROWS // (NY * NZ * NC)
SHARE = ROW_LOCAL // NX
BLOCK = 512
HALF = 768
TAIL = 16
PIECE = 32
F32, BF16 = jnp.float32, jnp.bfloat16
SIZES = {"y": NY, "z": NZ, "c": NC, "x": NX}
VMEM = pl.BlockSpec(memory_space=pltpu.VMEM)
SMEM = pl.BlockSpec(memory_space=pltpu.SMEM)
PARAMS = pltpu.CompilerParams(vmem_limit_bytes=20 * 1024 * 1024)
HIGH = lax.Precision.HIGHEST


def shift(x, axis, k):
    n = SIZES[axis]
    return lax.ppermute(x, axis, [(i, (i + k) % n) for i in range(n)])


def spread(x, axes, n):
    full = jnp.broadcast_to(x[None], (n,) + x.shape)
    return lax.all_to_all(full, axes, 0, 0, tiled=True)


def after(values, *first):
    n = len(values)
    return pl.pallas_call(
        lambda *refs: None,
        in_specs=[VMEM] * n + [pl.BlockSpec(memory_space=pl.ANY)] * len(first),
        out_specs=[VMEM] * n,
        out_shape=[jax.ShapeDtypeStruct(v.shape, v.dtype) for v in values],
        input_output_aliases={i: i for i in range(n)},
        compiler_params=PARAMS,
    )(*values, *first)


def prep_kernel(place, m_ref, g_ref, b_ref):
    b_ref[0] = (m_ref[...] + g_ref[...].astype(F32)).astype(BF16)


def prep(place, momentum, grad):
    spec = pl.BlockSpec((ROW_LOCAL, BLOCK), lambda k, s: (0, lax.rem(s[1] + k, NY)))
    return pl.pallas_call(
        prep_kernel,
        grid_spec=pltpu.PrefetchScalarGridSpec(
            num_scalar_prefetch=1,
            grid=(NY,),
            in_specs=[spec, spec],
            out_specs=pl.BlockSpec((1, ROW_LOCAL, BLOCK), lambda k, s: (k, 0, 0)),
        ),
        out_shape=jax.ShapeDtypeStruct((NY, ROW_LOCAL, BLOCK), BF16),
        compiler_params=PARAMS,
        cost_estimate=pl.CostEstimate(flops=10**6, bytes_accessed=16 * 2**20, transcendentals=0),
    )(place, momentum, grad)


def weave(place, mine, other, whole):
    c = place[2]
    each = NZ // len(mine)
    for z in range(NZ):
        rows = pl.ds(z % each * PIECE, PIECE)
        at = pl.multiple_of(z * 2 * PIECE + c * PIECE, PIECE)
        whole[pl.ds(at, PIECE), :] = mine[z // each][rows, :]
        at = pl.multiple_of(z * 2 * PIECE + (1 - c) * PIECE, PIECE)
        whole[pl.ds(at, PIECE), :] = other[z // each][rows, :]


def chunks_of(refs):
    return [refs[:1], refs[1:2], refs[2:4], refs[4:]]


def product_kernel(place, b_ref, *refs):
    mine, other, out = chunks_of(refs[:5]), chunks_of(refs[5:10]), refs[10:-2]
    whole, rows = refs[-2:]
    for k in range(NY):
        weave(place, mine[k], other[k], whole.at[k])
    total = jnp.dot(b_ref[0], whole[0], preferred_element_type=F32)
    for k in range(1, NY):
        total += jnp.dot(b_ref[k], whole[k], preferred_element_type=F32)
    rows[...] = total
    for k in range(NX):
        at = pl.multiple_of(lax.rem(place[0] + k, NX) * SHARE, SHARE)
        out[k][...] = rows[pl.ds(at, SHARE), :]


def product_of(place, b, mine, other):
    return pl.pallas_call(
        product_kernel,
        in_specs=[SMEM] + [VMEM] * (1 + len(mine) + len(other)),
        out_specs=[VMEM] * NX,
        out_shape=[jax.ShapeDtypeStruct((SHARE, RANK), F32)] * NX,
        scratch_shapes=[pltpu.VMEM((NY, BLOCK, RANK), BF16), pltpu.VMEM((ROW_LOCAL, RANK), F32)],
        compiler_params=PARAMS,
    )(place, b, *mine, *other)


def gram_kernel(place, own, before, top, low, behind, first, keep, give, product, whole):
    half = SHARE // 2
    for k, part in enumerate((own, before, None, behind)):
        at = pl.multiple_of(lax.rem(place[0] + k, NX) * SHARE, SHARE)
        if part is None:
            product[pl.ds(at, half), :] = top[...]
            product[pl.ds(at + half, half), :] = low[...]
        else:
            product[pl.ds(at, SHARE), :] = part[...]
    left, right = product[:, :256], product[:, 256:]
    for i, (a, b) in enumerate(((left, left), (right, left), (right, right))):
        g = lax.dot_general(a, b, (((0,), (0,)), ((), ())), precision=HIGH, preferred_element_type=F32)
        whole[pl.ds(i * 512, 256), :] = g[:, :128]
        whole[pl.ds(i * 512 + 256, 256), :] = g[:, 128:]
    keep[...] = whole[pl.ds(pl.multiple_of(place[2] * HALF, HALF), HALF), :]
    give[...] = whole[pl.ds(pl.multiple_of((1 - place[2]) * HALF, HALF), HALF), :]


def gram_of(place, shares, first):
    half = jax.ShapeDtypeStruct((HALF, 128), F32)
    return pl.pallas_call(
        gram_kernel,
        in_specs=[SMEM] + [VMEM] * (len(shares) + 1),
        out_specs=[VMEM] * 3,
        out_shape=[half, half, jax.ShapeDtypeStruct((ROW_LOCAL, RANK), F32)],
        scratch_shapes=[pltpu.VMEM((2 * HALF, 128), F32)],
        compiler_params=PARAMS,
    )(place, *shares, first)


def sum_spread_kernel(parts, *refs):
    total = jnp.sum(parts[...], axis=0)
    for i in range(refs[-1].shape[0]):
        refs[-1][i] = total


def sum_spread(parts, n, *first):
    return pl.pallas_call(
        sum_spread_kernel,
        in_specs=[VMEM] * (1 + len(first)),
        out_specs=VMEM,
        out_shape=jax.ShapeDtypeStruct((n,) + parts.shape[1:], F32),
        compiler_params=PARAMS,
    )(parts, *first)


def sum_kernel(n, *refs):
    refs[-1][...] = sum(v[...] for v in refs[1:n]) + refs[0][...]


def sum_after(values, *first):
    return pl.pallas_call(
        functools.partial(sum_kernel, len(values)),
        in_specs=[VMEM] * (len(values) + len(first)),
        out_specs=VMEM,
        out_shape=jax.ShapeDtypeStruct(values[0].shape, F32),
        compiler_params=PARAMS,
    )(*values, *first)


def row_of(v, j):
    return jnp.broadcast_to(v[j : j + 1, :], v.shape)


def fdot(a, b, tb=False):
    dims = (((1,), (1 if tb else 0,)), ((), ()))
    return lax.dot_general(a, b, dims, precision=HIGH, preferred_element_type=F32)


def diag_inverse(m_ref, w_ref, block=32):
    n = m_ref.shape[0]
    lane = lax.broadcasted_iota(jnp.int32, (8, n), 1)
    sub = lax.broadcasted_iota(jnp.int32, (8, n), 0)
    groups = block // 8
    for top in range(0, n, block):
        end = top + block
        group = [m_ref[top + 8 * g : top + 8 * g + 8, :] for g in range(groups)]
        for i in range(groups):
            o = top + 8 * i
            cols = [[jnp.broadcast_to(r[:, o + k : o + k + 1], (8, n)) for k in range(8)] for r in group]
            pivot = list(cols[i])
            panel = (lane >= o) & (lane < o + 8)
            rows = jnp.where(panel, jnp.where(lane - o == sub, 1.0, 0.0), group[i])
            done = jnp.zeros((8, n), F32)
            for j in range(8):
                d = row_of(pivot[j], j)
                inv = 1.0 / d
                at = sub == j
                row = row_of(rows, j)
                done = jnp.where(at, row * lax.rsqrt(d), done)
                row = row * inv
                rows = jnp.where(at, row, rows - pivot[j] * row)
                for k in range(j + 1, 8):
                    t = row_of(pivot[k], j) * inv
                    pivot[k] = jnp.where(at, t, pivot[k] - pivot[j] * t)
            w_ref[o : o + 8, :] = jnp.where(lane < o + 8, done, 0.0)
            z = [row_of(rows, k) for k in range(8)]
            for g in range(groups):
                if g == i:
                    group[g] = rows
                elif g > i or end < n:
                    v = jnp.where(panel, 0.0, group[g])
                    for k in range(8):
                        v = v - cols[g][k] * z[k]
                    group[g] = v
        if end < n:
            zeros = [jnp.zeros((size, n), F32) for size in (top, n - end) if size]
            solved = jnp.concatenate(zeros[:-1] + group + zeros[-1:], 0)
            below = m_ref[end:, :]
            at = lax.broadcasted_iota(jnp.int32, below.shape, 1)
            m_ref[end:, :] = jnp.where((at >= top) & (at < end), 0.0, below) - fdot(below, solved)


def factor_kernel(place, mine, other, w, a, m, d):
    c = place[2]
    for h in range(NC):
        part = jnp.where(c == h, mine[...], other[...])
        for q in range(3):
            at = h * 3 + q
            i, j = ((0, 0), (1, 0), (1, 1))[at // 2]
            cols = j * 256 + at % 2 * 128
            a[i * 256 : i * 256 + 256, cols : cols + 128] = part[q * 256 : q * 256 + 256]
    w[...] = jnp.zeros((RANK, RANK), F32)
    for k in range(RANK // 128):
        o, e = k * 128, k * 128 + 128
        m[...] = a[o:e, o:e]
        diag_inverse(m, d)
        wd = d[...]
        w[o:e, o:e] = wd
        if k:
            w[o:e, 0:o] = fdot(wd, w[o:e, 0:o])
        if e < RANK:
            low = fdot(a[e:, o:e], wd, tb=True)
            for at in range(0, RANK - e, 128):
                cols = slice(e + at, e + at + 128)
                a[e + at :, cols] = a[e + at :, cols] - fdot(low[at:], low[at : at + 128], tb=True)
            w[e:, 0:e] = w[e:, 0:e] - fdot(low, w[o:e, 0:e])


def factor_inverse(place, mine, other):
    return pl.pallas_call(
        factor_kernel,
        in_specs=[SMEM, VMEM, VMEM],
        out_specs=VMEM,
        out_shape=jax.ShapeDtypeStruct((RANK, RANK), F32),
        scratch_shapes=[pltpu.VMEM((RANK, RANK), F32)] + [pltpu.VMEM((128, 128), F32)] * 2,
        compiler_params=PARAMS,
        cost_estimate=pl.CostEstimate(flops=10**6, bytes_accessed=2**20, transcendentals=0),
    )(place, mine, other)


def orth_kernel(place, w_ref, *refs):
    prod, out, (p_factor, own) = refs[:3], refs[3:6], refs[6:]
    w_top, w_low = w_ref[:256, :256], w_ref[256:, :]
    for k in range(3):
        rows = prod[k][...]
        p = jnp.concatenate([fdot(rows[:, :256], w_top, tb=True), fdot(rows, w_low, tb=True)], 1)
        out[k][...] = p.astype(BF16)
        if k == 0:
            own[...] = p
            at = pl.multiple_of(place[0] * SHARE, SHARE)
            p_factor[...] = own[pl.ds(at, SHARE), :] * jnp.sqrt(F32(ROWS))


def orth_of(place, w, prod):
    return pl.pallas_call(
        orth_kernel,
        in_specs=[SMEM] + [VMEM] * 4,
        out_specs=[VMEM] * 4,
        out_shape=[jax.ShapeDtypeStruct((ROW_LOCAL, RANK), BF16)] * 3
        + [jax.ShapeDtypeStruct((SHARE, RANK), F32)],
        scratch_shapes=[pltpu.VMEM((ROW_LOCAL, RANK), F32)],
        compiler_params=PARAMS,
    )(place, w, *prod)


def near_right_kernel(*refs):
    total = None
    for p, b in zip(refs[:3], refs[3:6]):
        part = lax.dot_general(b[...], p[...], (((0,), (0,)), ((), ())), preferred_element_type=F32)
        total = part if total is None else total + part
    refs[6][...] = total


def near_right_of(p, b):
    return pl.pallas_call(
        near_right_kernel,
        in_specs=[VMEM] * 6,
        out_specs=VMEM,
        out_shape=jax.ShapeDtypeStruct((BLOCK, RANK), F32),
        compiler_params=PARAMS,
        cost_estimate=pl.CostEstimate(flops=10**9, bytes_accessed=4 * 2**20, transcendentals=0),
    )(*p, *b)


def right_kernel(place, near, p_top, p_low, b, keep, give, total):
    p = jnp.concatenate([p_top[...], p_low[...]], 0)
    part = lax.dot_general(b[...], p, (((0,), (0,)), ((), ())), preferred_element_type=F32)
    total[...] = near[...] + part
    c = place[2]
    for z in range(NZ):
        at = pl.multiple_of(z * 2 * PIECE + c * PIECE, PIECE)
        keep[pl.ds(z * PIECE, PIECE), :] = total[pl.ds(at, PIECE), :]
        at = pl.multiple_of(z * 2 * PIECE + (1 - c) * PIECE, PIECE)
        give[pl.ds(z * PIECE, PIECE), :] = total[pl.ds(at, PIECE), :]


def right_of(place, near, p, b):
    half = jax.ShapeDtypeStruct((NZ * PIECE, RANK), F32)
    return pl.pallas_call(
        right_kernel,
        in_specs=[SMEM] + [VMEM] * 4,
        out_specs=[VMEM] * 2,
        out_shape=[half, half],
        scratch_shapes=[pltpu.VMEM((BLOCK, RANK), F32)],
        compiler_params=PARAMS,
    )(place, near, *p, b)


def tail_of(power):
    high = power.astype(BF16)
    rest = power - high.astype(F32)
    mid = rest.astype(BF16)
    low = (rest - mid.astype(F32)).astype(BF16)
    sub = lax.broadcasted_iota(jnp.int32, (TAIL, RANK), 0)
    high, mid, low = (jnp.broadcast_to(v.astype(F32), (TAIL, RANK)) for v in (high, mid, low))
    tail = jnp.where(sub == 0, high, jnp.where(sub == 1, mid, low))
    return jnp.where(sub < 3, tail, 0.0).astype(BF16)


def rows_kernel(pieces, r_mine, out):
    r = jnp.sum(pieces[...], axis=0)
    r_mine[...] = r
    half = r.astype(BF16)
    tail = tail_of(jnp.sum(r * r, axis=0, keepdims=True))
    for i in range(NZ):
        out[i, :PIECE, :] = half
        out[i, PIECE:, :] = tail


def rows_of(pieces):
    return pl.pallas_call(
        rows_kernel,
        in_specs=[VMEM],
        out_specs=[VMEM] * 2,
        out_shape=[
            jax.ShapeDtypeStruct((PIECE, RANK), F32),
            jax.ShapeDtypeStruct((NZ, PIECE + TAIL, RANK), BF16),
        ],
        compiler_params=PARAMS,
    )(pieces)


def pack_kernel(rows, out):
    power = jnp.zeros((1, RANK), F32)
    for z in range(NZ):
        out[pl.ds(z * PIECE, PIECE), :] = rows[z, :PIECE, :]
        power += jnp.sum(rows[z, PIECE:, :].astype(F32), axis=0, keepdims=True)
    out[pl.ds(NZ * PIECE, TAIL), :] = tail_of(power)


def pack(rows):
    return pl.pallas_call(
        pack_kernel,
        in_specs=[VMEM],
        out_specs=VMEM,
        out_shape=jax.ShapeDtypeStruct((NZ * PIECE + TAIL, RANK), BF16),
        compiler_params=PARAMS,
    )(rows)


def power_kernel(*refs):
    power = jnp.zeros((1, RANK), F32)
    for v in refs[:-1]:
        power += jnp.sum(v[v.shape[0] - TAIL :, :].astype(F32), axis=0, keepdims=True)
    refs[-1][...] = power


def power_of(chunks):
    return pl.pallas_call(
        power_kernel,
        in_specs=[VMEM] * len(chunks),
        out_specs=VMEM,
        out_shape=jax.ShapeDtypeStruct((1, RANK), F32),
        compiler_params=PARAMS,
    )(*chunks)


def update_kernel(n, place, p_ref, *refs):
    count = sum(n)
    mine, other = refs[:count], refs[count : 2 * count]
    m_ref, g_ref, (out, done, whole) = refs[2 * count], refs[2 * count + 1], refs[-3:]
    done[...] = jnp.zeros_like(done)
    for k, parts in enumerate(n):
        at = slice(sum(n[:k]), sum(n[:k]) + parts)

        @pl.when(pl.program_id(0) == k)
        def _(at=at):
            weave(place, mine[at], other[at], whole)

    update = lax.dot_general(
        p_ref[...], whole[...], (((1,), (1,)), ((), ())), preferred_element_type=F32
    )
    mixed = m_ref[...] + g_ref[...].astype(F32)
    out[...] = mixed - DECAY * update


def update_of(place, p_own, mine, other, momentum, grad, first, step, before=None):
    count, parts = len(mine), tuple(len(v) for v in mine)
    n = sum(parts)
    mine, other = sum(mine, []), sum(other, [])
    spec = pl.BlockSpec((ROW_LOCAL, BLOCK), lambda k, s: (0, lax.rem(s[1] + first + step * k, NY)))
    more = [] if before is None else [before]
    return pl.pallas_call(
        functools.partial(update_kernel, parts),
        grid_spec=pltpu.PrefetchScalarGridSpec(
            num_scalar_prefetch=1,
            grid=(count,),
            in_specs=[VMEM] * (1 + 2 * n) + [spec, spec] + [pl.BlockSpec(memory_space=pl.ANY)] * len(more),
            out_specs=[spec, VMEM],
            scratch_shapes=[pltpu.VMEM((BLOCK, RANK), BF16)],
        ),
        out_shape=[
            jax.ShapeDtypeStruct((ROW_LOCAL, NY * BLOCK), F32),
            jax.ShapeDtypeStruct((8, 128), F32),
        ],
        input_output_aliases={4 + 2 * n: 0} if more else {},
        compiler_params=PARAMS,
        cost_estimate=pl.CostEstimate(flops=count * 2**28, bytes_accessed=count * 3 * 2**20, transcendentals=0),
    )(place, p_own, *mine, *other, momentum, grad, *more)


def halves(before, behind):
    h = NZ * PIECE // 2
    return [shift(before[:h], "y", -1), shift(behind[h:], "y", 1)]


def body(momentum, grad, q_basis):
    x, y, c = lax.axis_index("x"), lax.axis_index("y"), lax.axis_index("c")
    place = jnp.stack([x, y, c]).astype(jnp.int32)

    q_own = spread(q_basis.astype(BF16), "z", NZ).reshape(NZ * PIECE, RANK)
    b = prep(place, momentum, grad)
    q_before, q_behind = after([shift(q_own, "y", -1), shift(q_own, "y", 1)], b)
    q_mine = [q_own, q_before, *halves(q_before, q_behind), q_behind]
    q_other = [shift(v, "c", 1) for v in q_mine]
    partial = product_of(place, b, q_mine, q_other)

    partial = [partial[0]] + [shift(partial[k], "x", k) for k in range(1, NX)]
    b_col = [b[0]] + [shift(b[k], "y", k) for k in range(1, NY)]
    share = sum_after(partial, b_col[1], b_col[3])

    h = SHARE // 2
    before, behind = shift(share, "x", -1), shift(share, "x", 1)
    shares = [share, before, shift(before[:h], "x", -1), shift(behind[h:], "x", 1), behind]

    keep, give, product = gram_of(place, shares, b_col[2])
    parts = sum_after([keep, shift(give, "c", 1)]).reshape(NY * NZ, HALF // (NY * NZ), 128)
    part = sum_spread(lax.all_to_all(parts, ("y", "z"), 0, 0, tiled=True), NY * NZ)
    mine = lax.all_to_all(part, ("y", "z"), 0, 0, tiled=True).reshape(HALF, 128)
    (product,) = after([product], mine)
    prod = [product, shift(product, "y", 1), shift(product, "y", -1)]
    w = factor_inverse(place, mine, shift(mine, "c", 1))

    p_own, p_behind, p_before, p_factor = orth_of(place, w, prod)
    h = ROW_LOCAL // 2
    p_beyond = [shift(p_before[:h], "y", -1), shift(p_behind[h:], "y", 1)]
    near = near_right_of([p_own, p_behind, p_before], [b_col[0], b_col[1], b_col[3]])
    keep, give = right_of(place, near, p_beyond, b_col[2])
    right = keep + shift(give, "c", 1)
    pieces = lax.all_to_all(right.reshape(NZ, PIECE, RANK), "z", 0, 0, tiled=True)
    r_mine, rows = rows_of(pieces)
    r_own = pack(lax.all_to_all(rows, "z", 0, 0, tiled=True))
    r_other = shift(r_own, "c", 1)

    given = (momentum, grad)
    out, done = update_of(place, p_own, [[r_own]], [[r_other]], *given, 0, 1)
    before, behind = after([shift(r_own, "y", -1), shift(r_own, "y", 1)], done)
    beyond = halves(before, behind)
    others = [shift(v, "c", 1) for v in (before, behind)]
    out, done = update_of(
        place, p_own, [[before], [behind]], [[v] for v in others], *given, 1, 2, out
    )
    beyond = list(after(beyond, done))
    beyond_other = [shift(v, "c", 1) for v in beyond]
    out, _ = update_of(place, p_own, [beyond], [beyond_other], *given, 2, 1, out)

    power = power_of([r_own, r_other, before, behind, *others, beyond[1], beyond_other[1]])
    power = power + sum(shift(power, "x", k) for k in range(1, NX))
    q_next = r_mine * lax.rsqrt(power / COLS + 1e-06)
    return p_factor, q_next, out


def solution(mesh):
    inner = Mesh(np.asarray(mesh.devices).reshape(NY, NZ, NC, NX), ("y", "z", "c", "x"))
    row, col = ("y", "z", "c"), "x"
    in_specs = (P(row, col), P(row, col), P((col,) + row, None))
    out_specs = (P(row + (col,), None), P((col,) + row, None), P(row, col))
    return jax.shard_map(body, mesh=inner, in_specs=in_specs, out_specs=out_specs, check_vma=False)
```

```python
import functools

import jax
import jax.numpy as jnp
import numpy as np
from jax import lax
from jax.experimental import pallas as pl
from jax.experimental.pallas import tpu as pltpu
from jax.sharding import Mesh, PartitionSpec as P

ROWS = 28672
COLS = 8192
RANK = 512
DECAY = 0.05

NY, NZ, NC, NX = 4, 8, 2, 4
ROW_LOCAL = ROWS // (NY * NZ * NC)
SHARE = ROW_LOCAL // NX
BLOCK = 512
HALF = 768
TAIL = 16
PIECE = 32
F32, BF16 = jnp.float32, jnp.bfloat16
SIZES = {"y": NY, "z": NZ, "c": NC, "x": NX}
VMEM = pl.BlockSpec(memory_space=pltpu.VMEM)
SMEM = pl.BlockSpec(memory_space=pltpu.SMEM)
PARAMS = pltpu.CompilerParams(vmem_limit_bytes=20 * 1024 * 1024)
HIGH = lax.Precision.HIGHEST


def shift(x, axis, k):
    n = SIZES[axis]
    return lax.ppermute(x, axis, [(i, (i + k) % n) for i in range(n)])


def spread(x, axes, n):
    full = jnp.broadcast_to(x[None], (n,) + x.shape)
    return lax.all_to_all(full, axes, 0, 0, tiled=True)


def after(values, *first):
    n = len(values)
    return pl.pallas_call(
        lambda *refs: None,
        in_specs=[VMEM] * n + [pl.BlockSpec(memory_space=pl.ANY)] * len(first),
        out_specs=[VMEM] * n,
        out_shape=[jax.ShapeDtypeStruct(v.shape, v.dtype) for v in values],
        input_output_aliases={i: i for i in range(n)},
        compiler_params=PARAMS,
    )(*values, *first)


def prep_kernel(place, m_ref, g_ref, b_ref):
    b_ref[0] = (m_ref[...] + g_ref[...].astype(F32)).astype(BF16)


def prep(place, momentum, grad):
    spec = pl.BlockSpec((ROW_LOCAL, BLOCK), lambda k, s: (0, lax.rem(s[1] + k, NY)))
    return pl.pallas_call(
        prep_kernel,
        grid_spec=pltpu.PrefetchScalarGridSpec(
            num_scalar_prefetch=1,
            grid=(NY,),
            in_specs=[spec, spec],
            out_specs=pl.BlockSpec((1, ROW_LOCAL, BLOCK), lambda k, s: (k, 0, 0)),
        ),
        out_shape=jax.ShapeDtypeStruct((NY, ROW_LOCAL, BLOCK), BF16),
        compiler_params=PARAMS,
        cost_estimate=pl.CostEstimate(flops=10**6, bytes_accessed=16 * 2**20, transcendentals=0),
    )(place, momentum, grad)


def weave(place, mine, other, whole):
    c = place[2]
    each = NZ // len(mine)
    for z in range(NZ):
        rows = pl.ds(z % each * PIECE, PIECE)
        at = pl.multiple_of(z * 2 * PIECE + c * PIECE, PIECE)
        whole[pl.ds(at, PIECE), :] = mine[z // each][rows, :]
        at = pl.multiple_of(z * 2 * PIECE + (1 - c) * PIECE, PIECE)
        whole[pl.ds(at, PIECE), :] = other[z // each][rows, :]


def chunks_of(refs):
    return [refs[:1], refs[1:2], refs[2:4], refs[4:]]


def product_kernel(place, b_ref, *refs):
    mine, other, out = chunks_of(refs[:5]), chunks_of(refs[5:10]), refs[10:-2]
    whole, rows = refs[-2:]
    for k in range(NY):
        weave(place, mine[k], other[k], whole.at[k])
    total = jnp.dot(b_ref[0], whole[0], preferred_element_type=F32)
    for k in range(1, NY):
        total += jnp.dot(b_ref[k], whole[k], preferred_element_type=F32)
    rows[...] = total
    for k in range(NX):
        at = pl.multiple_of(lax.rem(place[0] + k, NX) * SHARE, SHARE)
        out[k][...] = rows[pl.ds(at, SHARE), :]


def product_of(place, b, mine, other):
    return pl.pallas_call(
        product_kernel,
        in_specs=[SMEM] + [VMEM] * (1 + len(mine) + len(other)),
        out_specs=[VMEM] * NX,
        out_shape=[jax.ShapeDtypeStruct((SHARE, RANK), F32)] * NX,
        scratch_shapes=[pltpu.VMEM((NY, BLOCK, RANK), BF16), pltpu.VMEM((ROW_LOCAL, RANK), F32)],
        compiler_params=PARAMS,
    )(place, b, *mine, *other)


def gram_kernel(place, p_ref, keep, give, whole):
    left, right = p_ref[:, :256], p_ref[:, 256:]
    for i, (a, b) in enumerate(((left, left), (right, left), (right, right))):
        g = lax.dot_general(a, b, (((0,), (0,)), ((), ())), precision=HIGH, preferred_element_type=F32)
        whole[pl.ds(i * 512, 256), :] = g[:, :128]
        whole[pl.ds(i * 512 + 256, 256), :] = g[:, 128:]
    keep[...] = whole[pl.ds(pl.multiple_of(place[2] * HALF, HALF), HALF), :]
    give[...] = whole[pl.ds(pl.multiple_of((1 - place[2]) * HALF, HALF), HALF), :]


def gram_of(place, share):
    half = jax.ShapeDtypeStruct((HALF, 128), F32)
    return pl.pallas_call(
        gram_kernel,
        in_specs=[SMEM, VMEM],
        out_specs=[VMEM] * 2,
        out_shape=[half, half],
        scratch_shapes=[pltpu.VMEM((2 * HALF, 128), F32)],
        compiler_params=PARAMS,
    )(place, share)


def join_kernel(place, own, before, top, low, behind, *refs):
    half, product = SHARE // 2, refs[-1]
    for k, part in enumerate((own, before, None, behind)):
        at = pl.multiple_of(lax.rem(place[0] + k, NX) * SHARE, SHARE)
        if part is None:
            product[pl.ds(at, half), :] = top[...]
            product[pl.ds(at + half, half), :] = low[...]
        else:
            product[pl.ds(at, SHARE), :] = part[...]


def join(place, shares, *first):
    return pl.pallas_call(
        join_kernel,
        in_specs=[SMEM] + [VMEM] * (len(shares) + len(first)),
        out_specs=VMEM,
        out_shape=jax.ShapeDtypeStruct((ROW_LOCAL, RANK), F32),
        compiler_params=PARAMS,
    )(place, *shares, *first)


def sum_spread_kernel(parts, *refs):
    total = jnp.sum(parts[...], axis=0)
    for i in range(refs[-1].shape[0]):
        refs[-1][i] = total


def sum_spread(parts, n, *first):
    return pl.pallas_call(
        sum_spread_kernel,
        in_specs=[VMEM] * (1 + len(first)),
        out_specs=VMEM,
        out_shape=jax.ShapeDtypeStruct((n,) + parts.shape[1:], F32),
        compiler_params=PARAMS,
    )(parts, *first)


def sum_kernel(n, *refs):
    refs[-1][...] = sum(v[...] for v in refs[1:n]) + refs[0][...]


def sum_after(values, *first):
    return pl.pallas_call(
        functools.partial(sum_kernel, len(values)),
        in_specs=[VMEM] * (len(values) + len(first)),
        out_specs=VMEM,
        out_shape=jax.ShapeDtypeStruct(values[0].shape, F32),
        compiler_params=PARAMS,
    )(*values, *first)


def row_of(v, j):
    return jnp.broadcast_to(v[j : j + 1, :], v.shape)


def fdot(a, b, tb=False):
    dims = (((1,), (1 if tb else 0,)), ((), ()))
    return lax.dot_general(a, b, dims, precision=HIGH, preferred_element_type=F32)


def diag_inverse(m_ref, w_ref, block=32):
    n = m_ref.shape[0]
    lane = lax.broadcasted_iota(jnp.int32, (8, n), 1)
    sub = lax.broadcasted_iota(jnp.int32, (8, n), 0)
    groups = block // 8
    for top in range(0, n, block):
        end = top + block
        group = [m_ref[top + 8 * g : top + 8 * g + 8, :] for g in range(groups)]
        for i in range(groups):
            o = top + 8 * i
            cols = [[jnp.broadcast_to(r[:, o + k : o + k + 1], (8, n)) for k in range(8)] for r in group]
            pivot = list(cols[i])
            panel = (lane >= o) & (lane < o + 8)
            rows = jnp.where(panel, jnp.where(lane - o == sub, 1.0, 0.0), group[i])
            done = jnp.zeros((8, n), F32)
            for j in range(8):
                d = row_of(pivot[j], j)
                inv = 1.0 / d
                at = sub == j
                row = row_of(rows, j)
                done = jnp.where(at, row * lax.rsqrt(d), done)
                row = row * inv
                rows = jnp.where(at, row, rows - pivot[j] * row)
                for k in range(j + 1, 8):
                    t = row_of(pivot[k], j) * inv
                    pivot[k] = jnp.where(at, t, pivot[k] - pivot[j] * t)
            w_ref[o : o + 8, :] = jnp.where(lane < o + 8, done, 0.0)
            z = [row_of(rows, k) for k in range(8)]
            for g in range(groups):
                if g == i:
                    group[g] = rows
                elif g > i or end < n:
                    v = jnp.where(panel, 0.0, group[g])
                    for k in range(8):
                        v = v - cols[g][k] * z[k]
                    group[g] = v
        if end < n:
            zeros = [jnp.zeros((size, n), F32) for size in (top, n - end) if size]
            solved = jnp.concatenate(zeros[:-1] + group + zeros[-1:], 0)
            below = m_ref[end:, :]
            at = lax.broadcasted_iota(jnp.int32, below.shape, 1)
            m_ref[end:, :] = jnp.where((at >= top) & (at < end), 0.0, below) - fdot(below, solved)


def factor_kernel(place, mine, other, w, a, m, d):
    c = place[2]
    for h in range(NC):
        part = jnp.where(c == h, mine[...], other[...])
        for q in range(3):
            at = h * 3 + q
            i, j = ((0, 0), (1, 0), (1, 1))[at // 2]
            cols = j * 256 + at % 2 * 128
            a[i * 256 : i * 256 + 256, cols : cols + 128] = part[q * 256 : q * 256 + 256]
    w[...] = jnp.zeros((RANK, RANK), F32)
    for k in range(RANK // 128):
        o, e = k * 128, k * 128 + 128
        m[...] = a[o:e, o:e]
        diag_inverse(m, d)
        wd = d[...]
        w[o:e, o:e] = wd
        if k:
            w[o:e, 0:o] = fdot(wd, w[o:e, 0:o])
        if e < RANK:
            low = fdot(a[e:, o:e], wd, tb=True)
            for at in range(0, RANK - e, 128):
                cols = slice(e + at, e + at + 128)
                a[e + at :, cols] = a[e + at :, cols] - fdot(low[at:], low[at : at + 128], tb=True)
            w[e:, 0:e] = w[e:, 0:e] - fdot(low, w[o:e, 0:e])


def factor_inverse(place, mine, other):
    return pl.pallas_call(
        factor_kernel,
        in_specs=[SMEM, VMEM, VMEM],
        out_specs=VMEM,
        out_shape=jax.ShapeDtypeStruct((RANK, RANK), F32),
        scratch_shapes=[pltpu.VMEM((RANK, RANK), F32)] + [pltpu.VMEM((128, 128), F32)] * 2,
        compiler_params=PARAMS,
        cost_estimate=pl.CostEstimate(flops=10**6, bytes_accessed=2**20, transcendentals=0),
    )(place, mine, other)


def orth_kernel(place, w_ref, *refs):
    prod, out, (p_factor, own) = refs[:3], refs[3:6], refs[6:]
    w_top, w_low = w_ref[:256, :256], w_ref[256:, :]
    for k in range(3):
        rows = prod[k][...]
        p = jnp.concatenate([fdot(rows[:, :256], w_top, tb=True), fdot(rows, w_low, tb=True)], 1)
        out[k][...] = p.astype(BF16)
        if k == 0:
            own[...] = p
            at = pl.multiple_of(place[0] * SHARE, SHARE)
            p_factor[...] = own[pl.ds(at, SHARE), :] * jnp.sqrt(F32(ROWS))


def orth_of(place, w, prod):
    return pl.pallas_call(
        orth_kernel,
        in_specs=[SMEM] + [VMEM] * 4,
        out_specs=[VMEM] * 4,
        out_shape=[jax.ShapeDtypeStruct((ROW_LOCAL, RANK), BF16)] * 3
        + [jax.ShapeDtypeStruct((SHARE, RANK), F32)],
        scratch_shapes=[pltpu.VMEM((ROW_LOCAL, RANK), F32)],
        compiler_params=PARAMS,
    )(place, w, *prod)


def near_right_kernel(*refs):
    total = None
    for p, b in zip(refs[:3], refs[3:6]):
        part = lax.dot_general(b[...], p[...], (((0,), (0,)), ((), ())), preferred_element_type=F32)
        total = part if total is None else total + part
    refs[6][...] = total


def near_right_of(p, b):
    return pl.pallas_call(
        near_right_kernel,
        in_specs=[VMEM] * 6,
        out_specs=VMEM,
        out_shape=jax.ShapeDtypeStruct((BLOCK, RANK), F32),
        compiler_params=PARAMS,
        cost_estimate=pl.CostEstimate(flops=10**9, bytes_accessed=4 * 2**20, transcendentals=0),
    )(*p, *b)


def right_kernel(place, near, p_top, p_low, b, keep, give, total):
    p = jnp.concatenate([p_top[...], p_low[...]], 0)
    part = lax.dot_general(b[...], p, (((0,), (0,)), ((), ())), preferred_element_type=F32)
    total[...] = near[...] + part
    c = place[2]
    for z in range(NZ):
        at = pl.multiple_of(z * 2 * PIECE + c * PIECE, PIECE)
        keep[pl.ds(z * PIECE, PIECE), :] = total[pl.ds(at, PIECE), :]
        at = pl.multiple_of(z * 2 * PIECE + (1 - c) * PIECE, PIECE)
        give[pl.ds(z * PIECE, PIECE), :] = total[pl.ds(at, PIECE), :]


def right_of(place, near, p, b):
    half = jax.ShapeDtypeStruct((NZ * PIECE, RANK), F32)
    return pl.pallas_call(
        right_kernel,
        in_specs=[SMEM] + [VMEM] * 4,
        out_specs=[VMEM] * 2,
        out_shape=[half, half],
        scratch_shapes=[pltpu.VMEM((BLOCK, RANK), F32)],
        compiler_params=PARAMS,
    )(place, near, *p, b)


def tail_of(power):
    high = power.astype(BF16)
    rest = power - high.astype(F32)
    mid = rest.astype(BF16)
    low = (rest - mid.astype(F32)).astype(BF16)
    sub = lax.broadcasted_iota(jnp.int32, (TAIL, RANK), 0)
    high, mid, low = (jnp.broadcast_to(v.astype(F32), (TAIL, RANK)) for v in (high, mid, low))
    tail = jnp.where(sub == 0, high, jnp.where(sub == 1, mid, low))
    return jnp.where(sub < 3, tail, 0.0).astype(BF16)


def rows_kernel(pieces, r_mine, out):
    r = jnp.sum(pieces[...], axis=0)
    r_mine[...] = r
    half = r.astype(BF16)
    tail = tail_of(jnp.sum(r * r, axis=0, keepdims=True))
    for i in range(NZ):
        out[i, :PIECE, :] = half
        out[i, PIECE:, :] = tail


def rows_of(pieces):
    return pl.pallas_call(
        rows_kernel,
        in_specs=[VMEM],
        out_specs=[VMEM] * 2,
        out_shape=[
            jax.ShapeDtypeStruct((PIECE, RANK), F32),
            jax.ShapeDtypeStruct((NZ, PIECE + TAIL, RANK), BF16),
        ],
        compiler_params=PARAMS,
    )(pieces)


def pack_kernel(rows, out):
    power = jnp.zeros((1, RANK), F32)
    for z in range(NZ):
        out[pl.ds(z * PIECE, PIECE), :] = rows[z, :PIECE, :]
        power += jnp.sum(rows[z, PIECE:, :].astype(F32), axis=0, keepdims=True)
    out[pl.ds(NZ * PIECE, TAIL), :] = tail_of(power)


def pack(rows):
    return pl.pallas_call(
        pack_kernel,
        in_specs=[VMEM],
        out_specs=VMEM,
        out_shape=jax.ShapeDtypeStruct((NZ * PIECE + TAIL, RANK), BF16),
        compiler_params=PARAMS,
    )(rows)


def power_kernel(*refs):
    power = jnp.zeros((1, RANK), F32)
    for v in refs[:-1]:
        power += jnp.sum(v[v.shape[0] - TAIL :, :].astype(F32), axis=0, keepdims=True)
    refs[-1][...] = power


def power_of(chunks):
    return pl.pallas_call(
        power_kernel,
        in_specs=[VMEM] * len(chunks),
        out_specs=VMEM,
        out_shape=jax.ShapeDtypeStruct((1, RANK), F32),
        compiler_params=PARAMS,
    )(*chunks)


def update_kernel(n, place, p_ref, *refs):
    count = sum(n)
    mine, other = refs[:count], refs[count : 2 * count]
    m_ref, g_ref, (out, done, whole) = refs[2 * count], refs[2 * count + 1], refs[-3:]
    done[...] = jnp.zeros_like(done)
    for k, parts in enumerate(n):
        at = slice(sum(n[:k]), sum(n[:k]) + parts)

        @pl.when(pl.program_id(0) == k)
        def _(at=at):
            weave(place, mine[at], other[at], whole)

    update = lax.dot_general(
        p_ref[...], whole[...], (((1,), (1,)), ((), ())), preferred_element_type=F32
    )
    mixed = m_ref[...] + g_ref[...].astype(F32)
    out[...] = mixed - DECAY * update


def update_of(place, p_own, mine, other, momentum, grad, first, step, before=None):
    count, parts = len(mine), tuple(len(v) for v in mine)
    n = sum(parts)
    mine, other = sum(mine, []), sum(other, [])
    spec = pl.BlockSpec((ROW_LOCAL, BLOCK), lambda k, s: (0, lax.rem(s[1] + first + step * k, NY)))
    more = [] if before is None else [before]
    return pl.pallas_call(
        functools.partial(update_kernel, parts),
        grid_spec=pltpu.PrefetchScalarGridSpec(
            num_scalar_prefetch=1,
            grid=(count,),
            in_specs=[VMEM] * (1 + 2 * n) + [spec, spec] + [pl.BlockSpec(memory_space=pl.ANY)] * len(more),
            out_specs=[spec, VMEM],
            scratch_shapes=[pltpu.VMEM((BLOCK, RANK), BF16)],
        ),
        out_shape=[
            jax.ShapeDtypeStruct((ROW_LOCAL, NY * BLOCK), F32),
            jax.ShapeDtypeStruct((8, 128), F32),
        ],
        input_output_aliases={4 + 2 * n: 0} if more else {},
        compiler_params=PARAMS,
        cost_estimate=pl.CostEstimate(flops=count * 2**28, bytes_accessed=count * 3 * 2**20, transcendentals=0),
    )(place, p_own, *mine, *other, momentum, grad, *more)


def halves(before, behind):
    h = NZ * PIECE // 2
    return [shift(before[:h], "y", -1), shift(behind[h:], "y", 1)]


def body(momentum, grad, q_basis):
    x, y, c = lax.axis_index("x"), lax.axis_index("y"), lax.axis_index("c")
    place = jnp.stack([x, y, c]).astype(jnp.int32)

    q_own = spread(q_basis.astype(BF16), "z", NZ).reshape(NZ * PIECE, RANK)
    b = prep(place, momentum, grad)
    q_before, q_behind = after([shift(q_own, "y", -1), shift(q_own, "y", 1)], b)
    q_mine = [q_own, q_before, *halves(q_before, q_behind), q_behind]
    q_other = [shift(v, "c", 1) for v in q_mine]
    partial = product_of(place, b, q_mine, q_other)

    partial = [partial[0]] + [shift(partial[k], "x", k) for k in range(1, NX)]
    b_behind, b_before = shift(b[1], "y", 1), shift(b[3], "y", 3)
    (b_far,) = after([b[2]], b_behind, b_before)
    b_col = [b[0], b_behind, shift(b_far, "y", 2), b_before]
    share = sum_after(partial, b_col[1], b_col[3])

    keep, give = gram_of(place, share)
    parts = sum_after([keep, shift(give, "c", 1)], b_col[2]).reshape(NY * NX, HALF // (NY * NX), 128)
    part = sum_spread(lax.all_to_all(parts, ("y", "x"), 0, 0, tiled=True), NZ)
    (sent,) = after([share], part)
    before, behind = shift(sent, "x", -1), shift(sent, "x", 1)
    part = sum_spread(lax.all_to_all(part, "z", 0, 0, tiled=True), NY * NX, before, behind)
    mine = lax.all_to_all(part, ("y", "x"), 0, 0, tiled=True).reshape(HALF, 128)
    h = SHARE // 2
    shares = [sent, before, shift(before[:h], "x", -1), shift(behind[h:], "x", 1), behind]
    product = join(place, shares, mine)
    prod = [product, shift(product, "y", 1), shift(product, "y", -1)]
    w = factor_inverse(place, mine, shift(mine, "c", 1))

    p_own, p_behind, p_before, p_factor = orth_of(place, w, prod)
    h = ROW_LOCAL // 2
    p_beyond = [shift(p_before[:h], "y", -1), shift(p_behind[h:], "y", 1)]
    near = near_right_of([p_own, p_behind, p_before], [b_col[0], b_col[1], b_col[3]])
    keep, give = right_of(place, near, p_beyond, b_col[2])
    right = keep + shift(give, "c", 1)
    pieces = lax.all_to_all(right.reshape(NZ, PIECE, RANK), "z", 0, 0, tiled=True)
    r_mine, rows = rows_of(pieces)
    r_own = pack(lax.all_to_all(rows, "z", 0, 0, tiled=True))
    r_other = shift(r_own, "c", 1)

    given = (momentum, grad)
    out, done = update_of(place, p_own, [[r_own]], [[r_other]], *given, 0, 1)
    mine = list(after([shift(r_own, "y", -k) for k in range(1, NY)], done))
    other = [shift(v, "c", 1) for v in mine]
    power = power_of([r_own, r_other, *mine, *other])
    power = power + sum(shift(power, "x", k) for k in range(1, NX))
    out, _ = update_of(place, p_own, [[v] for v in mine], [[v] for v in other], *given, 1, 1, out)
    q_next = r_mine * lax.rsqrt(power / COLS + 1e-06)
    return p_factor, q_next, out


def solution(mesh):
    inner = Mesh(np.asarray(mesh.devices).reshape(NY, NZ, NC, NX), ("y", "z", "c", "x"))
    row, col = ("y", "z", "c"), "x"
    in_specs = (P(row, col), P(row, col), P((col,) + row, None))
    out_specs = (P(row + (col,), None), P((col,) + row, None), P(row, col))
    return jax.shard_map(body, mesh=inner, in_specs=in_specs, out_specs=out_specs, check_vma=False)
```

```python
import functools

import jax
import jax.numpy as jnp
import numpy as np
from jax import lax
from jax.experimental import pallas as pl
from jax.experimental.pallas import tpu as pltpu
from jax.sharding import Mesh, PartitionSpec as P

ROWS = 28672
COLS = 8192
RANK = 512
DECAY = 0.05

NY, NZ, NC, NX = 4, 8, 2, 4
ROW_LOCAL = ROWS // (NY * NZ * NC)
SHARE = ROW_LOCAL // NX
BLOCK = 512
HALF = 768
TAIL = 16
PIECE = 32
F32, BF16 = jnp.float32, jnp.bfloat16
SIZES = {"y": NY, "z": NZ, "c": NC, "x": NX}
VMEM = pl.BlockSpec(memory_space=pltpu.VMEM)
SMEM = pl.BlockSpec(memory_space=pltpu.SMEM)
PARAMS = pltpu.CompilerParams(vmem_limit_bytes=20 * 1024 * 1024)
HIGH = lax.Precision.HIGHEST


def shift(x, axis, k):
    n = SIZES[axis]
    return lax.ppermute(x, axis, [(i, (i + k) % n) for i in range(n)])


def spread(x, axes, n):
    full = jnp.broadcast_to(x[None], (n,) + x.shape)
    return lax.all_to_all(full, axes, 0, 0, tiled=True)


def after(values, *first):
    n = len(values)
    return pl.pallas_call(
        lambda *refs: None,
        in_specs=[VMEM] * n + [pl.BlockSpec(memory_space=pl.ANY)] * len(first),
        out_specs=[VMEM] * n,
        out_shape=[jax.ShapeDtypeStruct(v.shape, v.dtype) for v in values],
        input_output_aliases={i: i for i in range(n)},
        compiler_params=PARAMS,
    )(*values, *first)


def prep_kernel(place, m_ref, g_ref, b_ref):
    b_ref[0] = (m_ref[...] + g_ref[...].astype(F32)).astype(BF16)


def prep(place, momentum, grad):
    spec = pl.BlockSpec((ROW_LOCAL, BLOCK), lambda k, s: (0, lax.rem(s[1] + k, NY)))
    return pl.pallas_call(
        prep_kernel,
        grid_spec=pltpu.PrefetchScalarGridSpec(
            num_scalar_prefetch=1,
            grid=(NY,),
            in_specs=[spec, spec],
            out_specs=pl.BlockSpec((1, ROW_LOCAL, BLOCK), lambda k, s: (k, 0, 0)),
        ),
        out_shape=jax.ShapeDtypeStruct((NY, ROW_LOCAL, BLOCK), BF16),
        compiler_params=PARAMS,
        cost_estimate=pl.CostEstimate(flops=10**6, bytes_accessed=16 * 2**20, transcendentals=0),
    )(place, momentum, grad)


def weave(place, mine, other, whole):
    c = place[2]
    each = NZ // len(mine)
    for z in range(NZ):
        rows = pl.ds(z % each * PIECE, PIECE)
        at = pl.multiple_of(z * 2 * PIECE + c * PIECE, PIECE)
        whole[pl.ds(at, PIECE), :] = mine[z // each][rows, :]
        at = pl.multiple_of(z * 2 * PIECE + (1 - c) * PIECE, PIECE)
        whole[pl.ds(at, PIECE), :] = other[z // each][rows, :]


def chunks_of(refs):
    return [refs[:1], refs[1:2], refs[2:4], refs[4:]]


def product_kernel(place, b_ref, *refs):
    mine, other, out = chunks_of(refs[:5]), chunks_of(refs[5:10]), refs[10:-2]
    whole, rows = refs[-2:]
    for k in range(NY):
        weave(place, mine[k], other[k], whole.at[k])
    total = jnp.dot(b_ref[0], whole[0], preferred_element_type=F32)
    for k in range(1, NY):
        total += jnp.dot(b_ref[k], whole[k], preferred_element_type=F32)
    rows[...] = total
    for k in range(NX):
        at = pl.multiple_of(lax.rem(place[0] + k, NX) * SHARE, SHARE)
        out[k][...] = rows[pl.ds(at, SHARE), :]


def product_of(place, b, mine, other):
    return pl.pallas_call(
        product_kernel,
        in_specs=[SMEM] + [VMEM] * (1 + len(mine) + len(other)),
        out_specs=[VMEM] * NX,
        out_shape=[jax.ShapeDtypeStruct((SHARE, RANK), F32)] * NX,
        scratch_shapes=[pltpu.VMEM((NY, BLOCK, RANK), BF16), pltpu.VMEM((ROW_LOCAL, RANK), F32)],
        compiler_params=PARAMS,
    )(place, b, *mine, *other)


def gram_kernel(place, p_ref, keep, give, whole):
    left, right = p_ref[:, :256], p_ref[:, 256:]
    for i, (a, b) in enumerate(((left, left), (right, left), (right, right))):
        g = lax.dot_general(a, b, (((0,), (0,)), ((), ())), precision=HIGH, preferred_element_type=F32)
        whole[pl.ds(i * 512, 256), :] = g[:, :128]
        whole[pl.ds(i * 512 + 256, 256), :] = g[:, 128:]
    keep[...] = whole[pl.ds(pl.multiple_of(place[2] * HALF, HALF), HALF), :]
    give[...] = whole[pl.ds(pl.multiple_of((1 - place[2]) * HALF, HALF), HALF), :]


def gram_of(place, share):
    half = jax.ShapeDtypeStruct((HALF, 128), F32)
    return pl.pallas_call(
        gram_kernel,
        in_specs=[SMEM, VMEM],
        out_specs=[VMEM] * 2,
        out_shape=[half, half],
        scratch_shapes=[pltpu.VMEM((2 * HALF, 128), F32)],
        compiler_params=PARAMS,
    )(place, share)


def join_kernel(place, own, before, top, low, behind, *refs):
    half, product = SHARE // 2, refs[-1]
    for k, part in enumerate((own, before, None, behind)):
        at = pl.multiple_of(lax.rem(place[0] + k, NX) * SHARE, SHARE)
        if part is None:
            product[pl.ds(at, half), :] = top[...]
            product[pl.ds(at + half, half), :] = low[...]
        else:
            product[pl.ds(at, SHARE), :] = part[...]


def join(place, shares, *first):
    return pl.pallas_call(
        join_kernel,
        in_specs=[SMEM] + [VMEM] * (len(shares) + len(first)),
        out_specs=VMEM,
        out_shape=jax.ShapeDtypeStruct((ROW_LOCAL, RANK), F32),
        compiler_params=PARAMS,
    )(place, *shares, *first)


def sum_spread_kernel(parts, *refs):
    total = jnp.sum(parts[...], axis=0)
    for i in range(refs[-1].shape[0]):
        refs[-1][i] = total


def sum_spread(parts, n, *first):
    return pl.pallas_call(
        sum_spread_kernel,
        in_specs=[VMEM] * (1 + len(first)),
        out_specs=VMEM,
        out_shape=jax.ShapeDtypeStruct((n,) + parts.shape[1:], F32),
        compiler_params=PARAMS,
    )(parts, *first)


def sum_kernel(n, *refs):
    refs[-1][...] = sum(v[...] for v in refs[1:n]) + refs[0][...]


def sum_after(values, *first):
    return pl.pallas_call(
        functools.partial(sum_kernel, len(values)),
        in_specs=[VMEM] * (len(values) + len(first)),
        out_specs=VMEM,
        out_shape=jax.ShapeDtypeStruct(values[0].shape, F32),
        compiler_params=PARAMS,
    )(*values, *first)


def row_of(v, j):
    return jnp.broadcast_to(v[j : j + 1, :], v.shape)


def fdot(a, b, tb=False):
    dims = (((1,), (1 if tb else 0,)), ((), ()))
    return lax.dot_general(a, b, dims, precision=HIGH, preferred_element_type=F32)


def diag_inverse(m_ref, w_ref, block=32):
    n = m_ref.shape[0]
    lane = lax.broadcasted_iota(jnp.int32, (8, n), 1)
    sub = lax.broadcasted_iota(jnp.int32, (8, n), 0)
    groups = block // 8
    for top in range(0, n, block):
        end = top + block
        group = [m_ref[top + 8 * g : top + 8 * g + 8, :] for g in range(groups)]
        for i in range(groups):
            o = top + 8 * i
            cols = [[jnp.broadcast_to(r[:, o + k : o + k + 1], (8, n)) for k in range(8)] for r in group]
            pivot = list(cols[i])
            panel = (lane >= o) & (lane < o + 8)
            rows = jnp.where(panel, jnp.where(lane - o == sub, 1.0, 0.0), group[i])
            done = jnp.zeros((8, n), F32)
            for j in range(8):
                d = row_of(pivot[j], j)
                inv = 1.0 / d
                at = sub == j
                row = row_of(rows, j)
                done = jnp.where(at, row * lax.rsqrt(d), done)
                row = row * inv
                rows = jnp.where(at, row, rows - pivot[j] * row)
                for k in range(j + 1, 8):
                    t = row_of(pivot[k], j) * inv
                    pivot[k] = jnp.where(at, t, pivot[k] - pivot[j] * t)
            w_ref[o : o + 8, :] = jnp.where(lane < o + 8, done, 0.0)
            z = [row_of(rows, k) for k in range(8)]
            for g in range(groups):
                if g == i:
                    group[g] = rows
                elif g > i or end < n:
                    v = jnp.where(panel, 0.0, group[g])
                    for k in range(8):
                        v = v - cols[g][k] * z[k]
                    group[g] = v
        if end < n:
            zeros = [jnp.zeros((size, n), F32) for size in (top, n - end) if size]
            solved = jnp.concatenate(zeros[:-1] + group + zeros[-1:], 0)
            below = m_ref[end:, :]
            at = lax.broadcasted_iota(jnp.int32, below.shape, 1)
            m_ref[end:, :] = jnp.where((at >= top) & (at < end), 0.0, below) - fdot(below, solved)


def factor_kernel(place, mine, other, w, a, m, d):
    c = place[2]
    for h in range(NC):
        part = jnp.where(c == h, mine[...], other[...])
        for q in range(3):
            at = h * 3 + q
            i, j = ((0, 0), (1, 0), (1, 1))[at // 2]
            cols = j * 256 + at % 2 * 128
            a[i * 256 : i * 256 + 256, cols : cols + 128] = part[q * 256 : q * 256 + 256]
    w[...] = jnp.zeros((RANK, RANK), F32)
    for k in range(RANK // 128):
        o, e = k * 128, k * 128 + 128
        m[...] = a[o:e, o:e]
        diag_inverse(m, d)
        wd = d[...]
        w[o:e, o:e] = wd
        if k:
            w[o:e, 0:o] = fdot(wd, w[o:e, 0:o])
        if e < RANK:
            low = fdot(a[e:, o:e], wd, tb=True)
            for at in range(0, RANK - e, 128):
                cols = slice(e + at, e + at + 128)
                a[e + at :, cols] = a[e + at :, cols] - fdot(low[at:], low[at : at + 128], tb=True)
            w[e:, 0:e] = w[e:, 0:e] - fdot(low, w[o:e, 0:e])


def factor_inverse(place, mine, other):
    return pl.pallas_call(
        factor_kernel,
        in_specs=[SMEM, VMEM, VMEM],
        out_specs=VMEM,
        out_shape=jax.ShapeDtypeStruct((RANK, RANK), F32),
        scratch_shapes=[pltpu.VMEM((RANK, RANK), F32)] + [pltpu.VMEM((128, 128), F32)] * 2,
        compiler_params=PARAMS,
        cost_estimate=pl.CostEstimate(flops=10**6, bytes_accessed=2**20, transcendentals=0),
    )(place, mine, other)


def orth(rows, w_ref):
    low = fdot(rows, w_ref[256:, :], tb=True)
    return jnp.concatenate([fdot(rows[:, :256], w_ref[:256, :256], tb=True), low], 1)


def passed_kernel(w_ref, before, behind, top, low):
    half = ROW_LOCAL // 2
    p = orth(jnp.concatenate([before[:half, :], behind[half:, :]], 0), w_ref).astype(BF16)
    top[...] = p[:half]
    low[...] = p[half:]


def passed_of(w, before, behind):
    return pl.pallas_call(
        passed_kernel,
        in_specs=[VMEM] * 3,
        out_specs=[VMEM] * 2,
        out_shape=[jax.ShapeDtypeStruct((ROW_LOCAL // 2, RANK), BF16)] * 2,
        compiler_params=PARAMS,
    )(w, before, behind)


def orth_kernel(place, w_ref, own, before, behind, top, low, b_own, b_before, b_behind, *out):
    half = ROW_LOCAL // 2
    p_own, p_factor, near, rows = out
    rows[...] = orth(own[...], w_ref)
    at = pl.multiple_of(place[0] * SHARE, SHARE)
    p_factor[...] = rows[pl.ds(at, SHARE), :] * jnp.sqrt(F32(ROWS))
    p = rows[...].astype(BF16)
    p_own[...] = p
    rest = orth(jnp.concatenate([before[half:, :], behind[:half, :]], 0), w_ref).astype(BF16)
    p_before = jnp.concatenate([top[...], rest[:half]], 0)
    p_behind = jnp.concatenate([rest[half:], low[...]], 0)
    dims = (((0,), (0,)), ((), ()))
    total = lax.dot_general(b_own[...], p, dims, preferred_element_type=F32)
    total += lax.dot_general(b_before[...], p_before, dims, preferred_element_type=F32)
    total += lax.dot_general(b_behind[...], p_behind, dims, preferred_element_type=F32)
    near[...] = total


def orth_of(place, w, prod, passed, b):
    return pl.pallas_call(
        orth_kernel,
        in_specs=[SMEM] + [VMEM] * 9,
        out_specs=[VMEM] * 3,
        out_shape=[
            jax.ShapeDtypeStruct((ROW_LOCAL, RANK), BF16),
            jax.ShapeDtypeStruct((SHARE, RANK), F32),
            jax.ShapeDtypeStruct((BLOCK, RANK), F32),
        ],
        scratch_shapes=[pltpu.VMEM((ROW_LOCAL, RANK), F32)],
        compiler_params=PARAMS,
        cost_estimate=pl.CostEstimate(flops=5 * 10**9, bytes_accessed=8 * 2**20, transcendentals=0),
    )(place, w, *prod, *passed, *b)


def right_kernel(place, near, p_top, p_low, b, keep, give, total):
    p = jnp.concatenate([p_top[...], p_low[...]], 0)
    part = lax.dot_general(b[...], p, (((0,), (0,)), ((), ())), preferred_element_type=F32)
    total[...] = near[...] + part
    c = place[2]
    for z in range(NZ):
        at = pl.multiple_of(z * 2 * PIECE + c * PIECE, PIECE)
        keep[pl.ds(z * PIECE, PIECE), :] = total[pl.ds(at, PIECE), :]
        at = pl.multiple_of(z * 2 * PIECE + (1 - c) * PIECE, PIECE)
        give[pl.ds(z * PIECE, PIECE), :] = total[pl.ds(at, PIECE), :]


def right_of(place, near, p, b):
    half = jax.ShapeDtypeStruct((NZ * PIECE, RANK), F32)
    return pl.pallas_call(
        right_kernel,
        in_specs=[SMEM] + [VMEM] * 4,
        out_specs=[VMEM] * 2,
        out_shape=[half, half],
        scratch_shapes=[pltpu.VMEM((BLOCK, RANK), F32)],
        compiler_params=PARAMS,
    )(place, near, *p, b)


def tail_of(power):
    high = power.astype(BF16)
    rest = power - high.astype(F32)
    mid = rest.astype(BF16)
    low = (rest - mid.astype(F32)).astype(BF16)
    sub = lax.broadcasted_iota(jnp.int32, (TAIL, RANK), 0)
    high, mid, low = (jnp.broadcast_to(v.astype(F32), (TAIL, RANK)) for v in (high, mid, low))
    tail = jnp.where(sub == 0, high, jnp.where(sub == 1, mid, low))
    return jnp.where(sub < 3, tail, 0.0).astype(BF16)


def rows_kernel(pieces, r_mine, out):
    r = jnp.sum(pieces[...], axis=0)
    r_mine[...] = r
    half = r.astype(BF16)
    tail = tail_of(jnp.sum(r * r, axis=0, keepdims=True))
    for i in range(NZ):
        out[i, :PIECE, :] = half
        out[i, PIECE:, :] = tail


def rows_of(pieces):
    return pl.pallas_call(
        rows_kernel,
        in_specs=[VMEM],
        out_specs=[VMEM] * 2,
        out_shape=[
            jax.ShapeDtypeStruct((PIECE, RANK), F32),
            jax.ShapeDtypeStruct((NZ, PIECE + TAIL, RANK), BF16),
        ],
        compiler_params=PARAMS,
    )(pieces)


def pack_kernel(rows, out):
    power = jnp.zeros((1, RANK), F32)
    for z in range(NZ):
        out[pl.ds(z * PIECE, PIECE), :] = rows[z, :PIECE, :]
        power += jnp.sum(rows[z, PIECE:, :].astype(F32), axis=0, keepdims=True)
    out[pl.ds(NZ * PIECE, TAIL), :] = tail_of(power)


def pack(rows):
    return pl.pallas_call(
        pack_kernel,
        in_specs=[VMEM],
        out_specs=VMEM,
        out_shape=jax.ShapeDtypeStruct((NZ * PIECE + TAIL, RANK), BF16),
        compiler_params=PARAMS,
    )(rows)


def power_kernel(*refs):
    power = jnp.zeros((1, RANK), F32)
    for v in refs[:-1]:
        power += jnp.sum(v[v.shape[0] - TAIL :, :].astype(F32), axis=0, keepdims=True)
    refs[-1][...] = power


def power_of(chunks):
    return pl.pallas_call(
        power_kernel,
        in_specs=[VMEM] * len(chunks),
        out_specs=VMEM,
        out_shape=jax.ShapeDtypeStruct((1, RANK), F32),
        compiler_params=PARAMS,
    )(*chunks)


def update_kernel(n, place, p_ref, *refs):
    count = sum(n)
    mine, other = refs[:count], refs[count : 2 * count]
    m_ref, g_ref, (out, done, whole) = refs[2 * count], refs[2 * count + 1], refs[-3:]
    done[...] = jnp.zeros_like(done)
    for k, parts in enumerate(n):
        at = slice(sum(n[:k]), sum(n[:k]) + parts)

        @pl.when(pl.program_id(0) == k)
        def _(at=at):
            weave(place, mine[at], other[at], whole)

    update = lax.dot_general(
        p_ref[...], whole[...], (((1,), (1,)), ((), ())), preferred_element_type=F32
    )
    mixed = m_ref[...] + g_ref[...].astype(F32)
    out[...] = mixed - DECAY * update


def update_of(place, p_own, mine, other, momentum, grad, first, step, before=None):
    count, parts = len(mine), tuple(len(v) for v in mine)
    n = sum(parts)
    mine, other = sum(mine, []), sum(other, [])
    spec = pl.BlockSpec((ROW_LOCAL, BLOCK), lambda k, s: (0, lax.rem(s[1] + first + step * k, NY)))
    more = [] if before is None else [before]
    return pl.pallas_call(
        functools.partial(update_kernel, parts),
        grid_spec=pltpu.PrefetchScalarGridSpec(
            num_scalar_prefetch=1,
            grid=(count,),
            in_specs=[VMEM] * (1 + 2 * n) + [spec, spec] + [pl.BlockSpec(memory_space=pl.ANY)] * len(more),
            out_specs=[spec, VMEM],
            scratch_shapes=[pltpu.VMEM((BLOCK, RANK), BF16)],
        ),
        out_shape=[
            jax.ShapeDtypeStruct((ROW_LOCAL, NY * BLOCK), F32),
            jax.ShapeDtypeStruct((8, 128), F32),
        ],
        input_output_aliases={4 + 2 * n: 0} if more else {},
        compiler_params=PARAMS,
        cost_estimate=pl.CostEstimate(flops=count * 2**28, bytes_accessed=count * 3 * 2**20, transcendentals=0),
    )(place, p_own, *mine, *other, momentum, grad, *more)


def halves(before, behind):
    h = NZ * PIECE // 2
    return [shift(before[:h], "y", -1), shift(behind[h:], "y", 1)]


def body(momentum, grad, q_basis):
    x, y, c = lax.axis_index("x"), lax.axis_index("y"), lax.axis_index("c")
    place = jnp.stack([x, y, c]).astype(jnp.int32)

    q_own = spread(q_basis.astype(BF16), "z", NZ).reshape(NZ * PIECE, RANK)
    b = prep(place, momentum, grad)
    q_before, q_behind = after([shift(q_own, "y", -1), shift(q_own, "y", 1)], b)
    q_mine = [q_own, q_before, *halves(q_before, q_behind), q_behind]
    q_other = [shift(v, "c", 1) for v in q_mine]
    partial = product_of(place, b, q_mine, q_other)

    partial = [partial[0]] + [shift(partial[k], "x", k) for k in range(1, NX)]
    b_behind, b_before = shift(b[1], "y", 1), shift(b[3], "y", 3)
    (b_far,) = after([b[2]], b_behind, b_before)
    b_col = [b[0], b_behind, shift(b_far, "y", 2), b_before]
    share = sum_after(partial, b_col[1], b_col[3])

    keep, give = gram_of(place, share)
    parts = sum_after([keep, shift(give, "c", 1)], b_col[2]).reshape(NY * NX, HALF // (NY * NX), 128)
    part = sum_spread(lax.all_to_all(parts, ("y", "x"), 0, 0, tiled=True), NZ)
    (sent,) = after([share], part)
    before, behind = shift(sent, "x", -1), shift(sent, "x", 1)
    part = sum_spread(lax.all_to_all(part, "z", 0, 0, tiled=True), NY * NX, before, behind)
    mine = lax.all_to_all(part, ("y", "x"), 0, 0, tiled=True).reshape(HALF, 128)
    h = SHARE // 2
    shares = [sent, before, shift(before[:h], "x", -1), shift(behind[h:], "x", 1), behind]
    product = join(place, shares, mine)
    prod = [product, shift(product, "y", 1), shift(product, "y", -1)]
    w = factor_inverse(place, mine, shift(mine, "c", 1))

    own, behind, before = prod
    passed = passed_of(w, before, behind)
    p_beyond = [shift(passed[0], "y", -1), shift(passed[1], "y", 1)]
    p_own, p_factor, near = orth_of(place, w, [own, before, behind], passed, [b_col[0], b_col[3], b_col[1]])
    keep, give = right_of(place, near, p_beyond, b_col[2])
    right = keep + shift(give, "c", 1)
    pieces = lax.all_to_all(right.reshape(NZ, PIECE, RANK), "z", 0, 0, tiled=True)
    r_mine, rows = rows_of(pieces)
    r_own = pack(lax.all_to_all(rows, "z", 0, 0, tiled=True))
    r_other = shift(r_own, "c", 1)

    given = (momentum, grad)
    out, done = update_of(place, p_own, [[r_own]], [[r_other]], *given, 0, 1)
    mine = list(after([shift(r_own, "y", -k) for k in range(1, NY)], done))
    other = [shift(v, "c", 1) for v in mine]
    power = power_of([r_own, r_other, *mine, *other])
    power = power + sum(shift(power, "x", k) for k in range(1, NX))
    out, _ = update_of(place, p_own, [[v] for v in mine], [[v] for v in other], *given, 1, 1, out)
    q_next = r_mine * lax.rsqrt(power / COLS + 1e-06)
    return p_factor, q_next, out


def solution(mesh):
    inner = Mesh(np.asarray(mesh.devices).reshape(NY, NZ, NC, NX), ("y", "z", "c", "x"))
    row, col = ("y", "z", "c"), "x"
    in_specs = (P(row, col), P(row, col), P((col,) + row, None))
    out_specs = (P(row + (col,), None), P((col,) + row, None), P(row, col))
    return jax.shard_map(body, mesh=inner, in_specs=in_specs, out_specs=out_specs, check_vma=False)
```

```python
import functools

import jax
import jax.numpy as jnp
import numpy as np
from jax import lax
from jax.experimental import pallas as pl
from jax.experimental.pallas import tpu as pltpu
from jax.sharding import Mesh, PartitionSpec as P

ROWS = 28672
COLS = 8192
RANK = 512
DECAY = 0.05

NY, NZ, NC, NX = 4, 8, 2, 4
ROW_LOCAL = ROWS // (NY * NZ * NC)
SHARE = ROW_LOCAL // NX
BLOCK = 512
HALF = 768
TAIL = 16
PIECE = 32
F32, BF16 = jnp.float32, jnp.bfloat16
SIZES = {"y": NY, "z": NZ, "c": NC, "x": NX}
VMEM = pl.BlockSpec(memory_space=pltpu.VMEM)
SMEM = pl.BlockSpec(memory_space=pltpu.SMEM)
PARAMS = pltpu.CompilerParams(vmem_limit_bytes=20 * 1024 * 1024)
HIGH = lax.Precision.HIGHEST


def shift(x, axis, k):
    n = SIZES[axis]
    return lax.ppermute(x, axis, [(i, (i + k) % n) for i in range(n)])


def spread(x, axes, n):
    full = jnp.broadcast_to(x[None], (n,) + x.shape)
    return lax.all_to_all(full, axes, 0, 0, tiled=True)


def after(values, *first):
    n = len(values)
    return pl.pallas_call(
        lambda *refs: None,
        in_specs=[VMEM] * n + [pl.BlockSpec(memory_space=pl.ANY)] * len(first),
        out_specs=[VMEM] * n,
        out_shape=[jax.ShapeDtypeStruct(v.shape, v.dtype) for v in values],
        input_output_aliases={i: i for i in range(n)},
        compiler_params=PARAMS,
    )(*values, *first)


def prep_kernel(place, m_ref, g_ref, b_ref):
    b_ref[0] = (m_ref[...] + g_ref[...].astype(F32)).astype(BF16)


def prep(place, momentum, grad):
    spec = pl.BlockSpec((ROW_LOCAL, BLOCK), lambda k, s: (0, lax.rem(s[1] + k, NY)))
    return pl.pallas_call(
        prep_kernel,
        grid_spec=pltpu.PrefetchScalarGridSpec(
            num_scalar_prefetch=1,
            grid=(NY,),
            in_specs=[spec, spec],
            out_specs=pl.BlockSpec((1, ROW_LOCAL, BLOCK), lambda k, s: (k, 0, 0)),
        ),
        out_shape=jax.ShapeDtypeStruct((NY, ROW_LOCAL, BLOCK), BF16),
        compiler_params=PARAMS,
        cost_estimate=pl.CostEstimate(flops=10**6, bytes_accessed=16 * 2**20, transcendentals=0),
    )(place, momentum, grad)


def weave(place, mine, other, whole):
    c = place[2]
    each = NZ // len(mine)
    for z in range(NZ):
        rows = pl.ds(z % each * PIECE, PIECE)
        at = pl.multiple_of(z * 2 * PIECE + c * PIECE, PIECE)
        whole[pl.ds(at, PIECE), :] = mine[z // each][rows, :]
        at = pl.multiple_of(z * 2 * PIECE + (1 - c) * PIECE, PIECE)
        whole[pl.ds(at, PIECE), :] = other[z // each][rows, :]


def chunks_of(refs):
    return [refs[:1], refs[1:2], refs[2:4], refs[4:]]


def product_kernel(place, b_ref, *refs):
    mine, other, out = chunks_of(refs[:5]), chunks_of(refs[5:10]), refs[10:-2]
    whole, rows = refs[-2:]
    for k in range(NY):
        weave(place, mine[k], other[k], whole.at[k])
    total = jnp.dot(b_ref[0], whole[0], preferred_element_type=F32)
    for k in range(1, NY):
        total += jnp.dot(b_ref[k], whole[k], preferred_element_type=F32)
    rows[...] = total
    for k in range(NX):
        at = pl.multiple_of(lax.rem(place[0] + k, NX) * SHARE, SHARE)
        out[k][...] = rows[pl.ds(at, SHARE), :]


def product_of(place, b, mine, other):
    return pl.pallas_call(
        product_kernel,
        in_specs=[SMEM] + [VMEM] * (1 + len(mine) + len(other)),
        out_specs=[VMEM] * NX,
        out_shape=[jax.ShapeDtypeStruct((SHARE, RANK), F32)] * NX,
        scratch_shapes=[pltpu.VMEM((NY, BLOCK, RANK), BF16), pltpu.VMEM((ROW_LOCAL, RANK), F32)],
        compiler_params=PARAMS,
    )(place, b, *mine, *other)


def gram_kernel(place, p_ref, keep, give, whole):
    left, right = p_ref[:, :256], p_ref[:, 256:]
    for i, (a, b) in enumerate(((left, left), (right, left), (right, right))):
        g = lax.dot_general(a, b, (((0,), (0,)), ((), ())), precision=HIGH, preferred_element_type=F32)
        whole[pl.ds(i * 512, 256), :] = g[:, :128]
        whole[pl.ds(i * 512 + 256, 256), :] = g[:, 128:]
    keep[...] = whole[pl.ds(pl.multiple_of(place[2] * HALF, HALF), HALF), :]
    give[...] = whole[pl.ds(pl.multiple_of((1 - place[2]) * HALF, HALF), HALF), :]


def gram_of(place, share):
    half = jax.ShapeDtypeStruct((HALF, 128), F32)
    return pl.pallas_call(
        gram_kernel,
        in_specs=[SMEM, VMEM],
        out_specs=[VMEM] * 2,
        out_shape=[half, half],
        scratch_shapes=[pltpu.VMEM((2 * HALF, 128), F32)],
        compiler_params=PARAMS,
    )(place, share)


def join_kernel(place, own, before, top, low, behind, *refs):
    half, product = SHARE // 2, refs[-1]
    for k, part in enumerate((own, before, None, behind)):
        at = pl.multiple_of(lax.rem(place[0] + k, NX) * SHARE, SHARE)
        if part is None:
            product[pl.ds(at, half), :] = top[...]
            product[pl.ds(at + half, half), :] = low[...]
        else:
            product[pl.ds(at, SHARE), :] = part[...]


def join(place, shares, *first):
    return pl.pallas_call(
        join_kernel,
        in_specs=[SMEM] + [VMEM] * (len(shares) + len(first)),
        out_specs=VMEM,
        out_shape=jax.ShapeDtypeStruct((ROW_LOCAL, RANK), F32),
        compiler_params=PARAMS,
    )(place, *shares, *first)


def sum_spread_kernel(parts, *refs):
    total = jnp.sum(parts[...], axis=0)
    for i in range(refs[-1].shape[0]):
        refs[-1][i] = total


def sum_spread(parts, n, *first):
    return pl.pallas_call(
        sum_spread_kernel,
        in_specs=[VMEM] * (1 + len(first)),
        out_specs=VMEM,
        out_shape=jax.ShapeDtypeStruct((n,) + parts.shape[1:], F32),
        compiler_params=PARAMS,
    )(parts, *first)


def sum_kernel(n, *refs):
    refs[-1][...] = sum(v[...] for v in refs[1:n]) + refs[0][...]


def sum_after(values, *first):
    return pl.pallas_call(
        functools.partial(sum_kernel, len(values)),
        in_specs=[VMEM] * (len(values) + len(first)),
        out_specs=VMEM,
        out_shape=jax.ShapeDtypeStruct(values[0].shape, F32),
        compiler_params=PARAMS,
    )(*values, *first)


def row_of(v, j):
    return jnp.broadcast_to(v[j : j + 1, :], v.shape)


def fdot(a, b, tb=False):
    dims = (((1,), (1 if tb else 0,)), ((), ()))
    return lax.dot_general(a, b, dims, precision=HIGH, preferred_element_type=F32)


def diag_inverse(m_ref, w_ref, block=32):
    n = m_ref.shape[0]
    lane = lax.broadcasted_iota(jnp.int32, (8, n), 1)
    sub = lax.broadcasted_iota(jnp.int32, (8, n), 0)
    groups = block // 8
    for top in range(0, n, block):
        end = top + block
        group = [m_ref[top + 8 * g : top + 8 * g + 8, :] for g in range(groups)]
        for i in range(groups):
            o = top + 8 * i
            cols = [[jnp.broadcast_to(r[:, o + k : o + k + 1], (8, n)) for k in range(8)] for r in group]
            pivot = list(cols[i])
            panel = (lane >= o) & (lane < o + 8)
            rows = jnp.where(panel, jnp.where(lane - o == sub, 1.0, 0.0), group[i])
            done = jnp.zeros((8, n), F32)
            for j in range(8):
                d = row_of(pivot[j], j)
                inv = 1.0 / d
                at = sub == j
                row = row_of(rows, j)
                done = jnp.where(at, row * lax.rsqrt(d), done)
                row = row * inv
                rows = jnp.where(at, row, rows - pivot[j] * row)
                for k in range(j + 1, 8):
                    t = row_of(pivot[k], j) * inv
                    pivot[k] = jnp.where(at, t, pivot[k] - pivot[j] * t)
            w_ref[o : o + 8, :] = jnp.where(lane < o + 8, done, 0.0)
            z = [row_of(rows, k) for k in range(8)]
            for g in range(groups):
                if g == i:
                    group[g] = rows
                elif g > i or end < n:
                    v = jnp.where(panel, 0.0, group[g])
                    for k in range(8):
                        v = v - cols[g][k] * z[k]
                    group[g] = v
        if end < n:
            zeros = [jnp.zeros((size, n), F32) for size in (top, n - end) if size]
            solved = jnp.concatenate(zeros[:-1] + group + zeros[-1:], 0)
            below = m_ref[end:, :]
            at = lax.broadcasted_iota(jnp.int32, below.shape, 1)
            m_ref[end:, :] = jnp.where((at >= top) & (at < end), 0.0, below) - fdot(below, solved)


def factor_kernel(place, mine, other, w, a, m, d):
    c = place[2]
    for h in range(NC):
        part = jnp.where(c == h, mine[...], other[...])
        for q in range(3):
            at = h * 3 + q
            i, j = ((0, 0), (1, 0), (1, 1))[at // 2]
            cols = j * 256 + at % 2 * 128
            a[i * 256 : i * 256 + 256, cols : cols + 128] = part[q * 256 : q * 256 + 256]
    w[...] = jnp.zeros((RANK, RANK), F32)
    for k in range(RANK // 128):
        o, e = k * 128, k * 128 + 128
        m[...] = a[o:e, o:e]
        diag_inverse(m, d)
        wd = d[...]
        w[o:e, o:e] = wd
        if k:
            w[o:e, 0:o] = fdot(wd, w[o:e, 0:o])
        if e < RANK:
            low = fdot(a[e:, o:e], wd, tb=True)
            for at in range(0, RANK - e, 128):
                cols = slice(e + at, e + at + 128)
                a[e + at :, cols] = a[e + at :, cols] - fdot(low[at:], low[at : at + 128], tb=True)
            w[e:, 0:e] = w[e:, 0:e] - fdot(low, w[o:e, 0:e])


def factor_inverse(place, mine, other):
    return pl.pallas_call(
        factor_kernel,
        in_specs=[SMEM, VMEM, VMEM],
        out_specs=VMEM,
        out_shape=jax.ShapeDtypeStruct((RANK, RANK), F32),
        scratch_shapes=[pltpu.VMEM((RANK, RANK), F32)] + [pltpu.VMEM((128, 128), F32)] * 2,
        compiler_params=PARAMS,
        cost_estimate=pl.CostEstimate(flops=10**6, bytes_accessed=2**20, transcendentals=0),
    )(place, mine, other)


def orth(rows, w_ref):
    low = fdot(rows, w_ref[256:, :], tb=True)
    return jnp.concatenate([fdot(rows[:, :256], w_ref[:256, :256], tb=True), low], 1)


def passed_kernel(w_ref, before, behind, top, low):
    half = ROW_LOCAL // 2
    p = orth(jnp.concatenate([before[:half, :], behind[half:, :]], 0), w_ref).astype(BF16)
    top[...] = p[:half]
    low[...] = p[half:]


def passed_of(w, before, behind):
    return pl.pallas_call(
        passed_kernel,
        in_specs=[VMEM] * 3,
        out_specs=[VMEM] * 2,
        out_shape=[jax.ShapeDtypeStruct((ROW_LOCAL // 2, RANK), BF16)] * 2,
        compiler_params=PARAMS,
    )(w, before, behind)


def orth_kernel(place, w_ref, own, before, behind, top, low, b_own, b_before, b_behind, *out):
    half = ROW_LOCAL // 2
    p_own, p_factor, near, rows = out
    rows[...] = orth(own[...], w_ref)
    at = pl.multiple_of(place[0] * SHARE, SHARE)
    p_factor[...] = rows[pl.ds(at, SHARE), :] * jnp.sqrt(F32(ROWS))
    p = rows[...].astype(BF16)
    p_own[...] = p
    rest = orth(jnp.concatenate([before[half:, :], behind[:half, :]], 0), w_ref).astype(BF16)
    p_before = jnp.concatenate([top[...], rest[:half]], 0)
    p_behind = jnp.concatenate([rest[half:], low[...]], 0)
    dims = (((0,), (0,)), ((), ()))
    total = lax.dot_general(b_own[...], p, dims, preferred_element_type=F32)
    total += lax.dot_general(b_before[...], p_before, dims, preferred_element_type=F32)
    total += lax.dot_general(b_behind[...], p_behind, dims, preferred_element_type=F32)
    near[...] = total


def orth_of(place, w, prod, passed, b):
    return pl.pallas_call(
        orth_kernel,
        in_specs=[SMEM] + [VMEM] * 9,
        out_specs=[VMEM] * 3,
        out_shape=[
            jax.ShapeDtypeStruct((ROW_LOCAL, RANK), BF16),
            jax.ShapeDtypeStruct((SHARE, RANK), F32),
            jax.ShapeDtypeStruct((BLOCK, RANK), F32),
        ],
        scratch_shapes=[pltpu.VMEM((ROW_LOCAL, RANK), F32)],
        compiler_params=PARAMS,
        cost_estimate=pl.CostEstimate(flops=5 * 10**9, bytes_accessed=8 * 2**20, transcendentals=0),
    )(place, w, *prod, *passed, *b)


def right_kernel(place, near, p_top, p_low, b, keep, give, total):
    p = jnp.concatenate([p_top[...], p_low[...]], 0)
    part = lax.dot_general(b[...], p, (((0,), (0,)), ((), ())), preferred_element_type=F32)
    total[...] = near[...] + part
    c = place[2]
    for z in range(NZ):
        at = pl.multiple_of(z * 2 * PIECE + c * PIECE, PIECE)
        keep[pl.ds(z * PIECE, PIECE), :] = total[pl.ds(at, PIECE), :]
        at = pl.multiple_of(z * 2 * PIECE + (1 - c) * PIECE, PIECE)
        give[pl.ds(z * PIECE, PIECE), :] = total[pl.ds(at, PIECE), :]


def right_of(place, near, p, b):
    half = jax.ShapeDtypeStruct((NZ * PIECE, RANK), F32)
    return pl.pallas_call(
        right_kernel,
        in_specs=[SMEM] + [VMEM] * 4,
        out_specs=[VMEM] * 2,
        out_shape=[half, half],
        scratch_shapes=[pltpu.VMEM((BLOCK, RANK), F32)],
        compiler_params=PARAMS,
    )(place, near, *p, b)


def tail_of(power):
    high = power.astype(BF16)
    rest = power - high.astype(F32)
    mid = rest.astype(BF16)
    low = (rest - mid.astype(F32)).astype(BF16)
    sub = lax.broadcasted_iota(jnp.int32, (TAIL, RANK), 0)
    high, mid, low = (jnp.broadcast_to(v.astype(F32), (TAIL, RANK)) for v in (high, mid, low))
    tail = jnp.where(sub == 0, high, jnp.where(sub == 1, mid, low))
    return jnp.where(sub < 3, tail, 0.0).astype(BF16)


def rows_kernel(pieces, r_mine, out):
    r = jnp.sum(pieces[...], axis=0)
    r_mine[...] = r
    half = r.astype(BF16)
    tail = tail_of(jnp.sum(r * r, axis=0, keepdims=True))
    for i in range(NZ):
        out[i, :PIECE, :] = half
        out[i, PIECE:, :] = tail


def rows_of(pieces):
    return pl.pallas_call(
        rows_kernel,
        in_specs=[VMEM],
        out_specs=[VMEM] * 2,
        out_shape=[
            jax.ShapeDtypeStruct((PIECE, RANK), F32),
            jax.ShapeDtypeStruct((NZ, PIECE + TAIL, RANK), BF16),
        ],
        compiler_params=PARAMS,
    )(pieces)


def pack_kernel(rows, out):
    power = jnp.zeros((1, RANK), F32)
    for z in range(NZ):
        out[pl.ds(z * PIECE, PIECE), :] = rows[z, :PIECE, :]
        power += jnp.sum(rows[z, PIECE:, :].astype(F32), axis=0, keepdims=True)
    out[pl.ds(NZ * PIECE, TAIL), :] = tail_of(power)


def pack(rows):
    return pl.pallas_call(
        pack_kernel,
        in_specs=[VMEM],
        out_specs=VMEM,
        out_shape=jax.ShapeDtypeStruct((NZ * PIECE + TAIL, RANK), BF16),
        compiler_params=PARAMS,
    )(rows)


def power_kernel(*refs):
    power = jnp.zeros((1, RANK), F32)
    for v in refs[:-1]:
        power += jnp.sum(v[v.shape[0] - TAIL :, :].astype(F32), axis=0, keepdims=True)
    refs[-1][...] = power


def power_of(chunks):
    return pl.pallas_call(
        power_kernel,
        in_specs=[VMEM] * len(chunks),
        out_specs=VMEM,
        out_shape=jax.ShapeDtypeStruct((1, RANK), F32),
        compiler_params=PARAMS,
    )(*chunks)


def update_kernel(n, place, p_ref, *refs):
    count = sum(n)
    mine, other = refs[:count], refs[count : 2 * count]
    m_ref, g_ref, (out, done, whole) = refs[2 * count], refs[2 * count + 1], refs[-3:]
    done[...] = jnp.zeros_like(done)
    for k, parts in enumerate(n):
        at = slice(sum(n[:k]), sum(n[:k]) + parts)

        @pl.when(pl.program_id(0) == k)
        def _(at=at):
            weave(place, mine[at], other[at], whole)

    update = lax.dot_general(
        p_ref[...], whole[...], (((1,), (1,)), ((), ())), preferred_element_type=F32
    )
    mixed = m_ref[...] + g_ref[...].astype(F32)
    out[...] = mixed - DECAY * update


def update_of(place, p_own, mine, other, momentum, grad, first, step, before=None):
    count, parts = len(mine), tuple(len(v) for v in mine)
    n = sum(parts)
    mine, other = sum(mine, []), sum(other, [])
    spec = pl.BlockSpec((ROW_LOCAL, BLOCK), lambda k, s: (0, lax.rem(s[1] + first + step * k, NY)))
    more = [] if before is None else [before]
    return pl.pallas_call(
        functools.partial(update_kernel, parts),
        grid_spec=pltpu.PrefetchScalarGridSpec(
            num_scalar_prefetch=1,
            grid=(count,),
            in_specs=[VMEM] * (1 + 2 * n) + [spec, spec] + [pl.BlockSpec(memory_space=pl.ANY)] * len(more),
            out_specs=[spec, VMEM],
            scratch_shapes=[pltpu.VMEM((BLOCK, RANK), BF16)],
        ),
        out_shape=[
            jax.ShapeDtypeStruct((ROW_LOCAL, NY * BLOCK), F32),
            jax.ShapeDtypeStruct((8, 128), F32),
        ],
        input_output_aliases={4 + 2 * n: 0} if more else {},
        compiler_params=PARAMS,
        cost_estimate=pl.CostEstimate(flops=count * 2**28, bytes_accessed=count * 3 * 2**20, transcendentals=0),
    )(place, p_own, *mine, *other, momentum, grad, *more)


def halves(before, behind):
    h = NZ * PIECE // 2
    return [shift(before[:h], "y", -1), shift(behind[h:], "y", 1)]


def body(momentum, grad, q_basis):
    x, y, c = lax.axis_index("x"), lax.axis_index("y"), lax.axis_index("c")
    place = jnp.stack([x, y, c]).astype(jnp.int32)

    q_own = spread(q_basis.astype(BF16), "z", NZ).reshape(NZ * PIECE, RANK)
    b = prep(place, momentum, grad)
    q_before, q_behind = after([shift(q_own, "y", -1), shift(q_own, "y", 1)], b)
    q_mine = [q_own, q_before, *halves(q_before, q_behind), q_behind]
    q_other = [shift(v, "c", 1) for v in q_mine]
    partial = product_of(place, b, q_mine, q_other)

    partial = [partial[0]] + [shift(partial[k], "x", k) for k in range(1, NX)]
    b_behind, b_before = shift(b[1], "y", 1), shift(b[3], "y", 3)
    (b_far,) = after([b[2]], b_behind, b_before)
    b_col = [b[0], b_behind, shift(b_far, "y", 2), b_before]
    share = sum_after(partial, b_col[1], b_col[3])

    keep, give = gram_of(place, share)
    parts = sum_after([keep, shift(give, "c", 1)], b_col[2]).reshape(NY * NX, HALF // (NY * NX), 128)
    part = sum_spread(lax.all_to_all(parts, ("y", "x"), 0, 0, tiled=True), NZ)
    (sent,) = after([share], part)
    before, behind = shift(sent, "x", -1), shift(sent, "x", 1)
    part = sum_spread(lax.all_to_all(part, "z", 0, 0, tiled=True), NY * NX, before, behind)
    mine = lax.all_to_all(part, ("y", "x"), 0, 0, tiled=True).reshape(HALF, 128)
    h = SHARE // 2
    shares = [sent, before, shift(before[:h], "x", -1), shift(behind[h:], "x", 1), behind]
    (mine,) = after([mine], *shares[2:4])
    other = shift(mine, "c", 1)
    (product,) = after([join(place, shares, mine)], other)
    prod = [product, shift(product, "y", 1), shift(product, "y", -1)]
    w = factor_inverse(place, mine, other)

    own, behind, before = prod
    passed = passed_of(w, before, behind)
    p_beyond = [shift(passed[0], "y", -1), shift(passed[1], "y", 1)]
    p_own, p_factor, near = orth_of(place, w, [own, before, behind], passed, [b_col[0], b_col[3], b_col[1]])
    keep, give = right_of(place, near, p_beyond, b_col[2])
    right = keep + shift(give, "c", 1)
    pieces = lax.all_to_all(right.reshape(NZ, PIECE, RANK), "z", 0, 0, tiled=True)
    r_mine, rows = rows_of(pieces)
    r_own = pack(lax.all_to_all(rows, "z", 0, 0, tiled=True))
    r_other = shift(r_own, "c", 1)

    given = (momentum, grad)
    out, done = update_of(place, p_own, [[r_own]], [[r_other]], *given, 0, 1)
    mine = list(after([shift(r_own, "y", -k) for k in range(1, NY)], done))
    other = [shift(v, "c", 1) for v in mine]
    power = power_of([r_own, r_other, *mine, *other])
    power = power + sum(shift(power, "x", k) for k in range(1, NX))
    out, _ = update_of(place, p_own, [[v] for v in mine], [[v] for v in other], *given, 1, 1, out)
    q_next = r_mine * lax.rsqrt(power / COLS + 1e-06)
    return p_factor, q_next, out


def solution(mesh):
    inner = Mesh(np.asarray(mesh.devices).reshape(NY, NZ, NC, NX), ("y", "z", "c", "x"))
    row, col = ("y", "z", "c"), "x"
    in_specs = (P(row, col), P(row, col), P((col,) + row, None))
    out_specs = (P(row + (col,), None), P((col,) + row, None), P(row, col))
    return jax.shard_map(body, mesh=inner, in_specs=in_specs, out_specs=out_specs, check_vma=False)
```
